32 devices in a mesh: groups: 2 (over x), node: 8 (over z, y), lane: 2 (over core).
Axes of the slice: x: 2, y: 2, z: 4, core: 2. Of those that a mesh axis runs over, the one named last changes fastest.
Arguments:
- expert_hidden: bfloat16 [512, 8, 1024], P(('groups', 'node', 'lane')), parts along dimension 0, may hold values from -6 to 6
- gate_scores: float32 [512, 8], P(('groups', 'node', 'lane')), parts along dimension 0, may hold values from 0.05 to 1
- node_lists: int32 [512, 4], P(('groups', 'node', 'lane')), parts along dimension 0, may hold values from 0 to 7, all different within a row; in each aligned block of 16 rows (0 to 15, 16 to 31, ...) at most 8 rows name the same one
- expert_picks: int32 [512, 8], P(('groups', 'node', 'lane')), parts along dimension 0, may hold values from 0 to 7, as said below
- routed_down: bfloat16 [16, 1024, 3584], P(('node', 'lane')), may hold values from -0.1875 to 0.1875
- query_latent: bfloat16 [256, 64, 512], P(('groups', 'node', 'lane')), parts along dimension 0, may hold values from -6 to 6
- query_rope: bfloat16 [256, 4096], P(('groups', 'node', 'lane')), parts along dimension 0, may hold values from -100 to 100
- cache_latent: bfloat16 [256, 128, 512], P(('groups', 'node', 'lane')), parts along dimension 0, may hold values from -6 to 6
- cache_rope: bfloat16 [256, 64, 128], P(('groups', 'node', 'lane')), parts along dimension 0, may hold values from -6 to 6
- cache_lengths: int32 [256], P(('groups', 'node', 'lane')), parts along dimension 0, may hold values from 2 to 128, as said below
Outputs:
- moe_out: bfloat16 [512, 3584], P(('groups', 'node', 'lane')), parts along dimension 0
- context: bfloat16 [256, 64, 512], P(('groups', 'node', 'lane')), parts along dimension 0
The draws below stay inside these ranges and needn't reach their ends.
There are 2 independent parts, one for each index of `groups`. The reference program is written for one: setup_inputs(seed, part) draws one part's arguments, and reference() takes and returns one part's arrays. A program takes and returns all parts, laid end to end along the dimension named above; an argument that names none is the same for every part. Nothing has to cross between parts.
Inputs may be any that keep to these rules, and one draw needn't show every extreme that they name: `node_lists`: each row names 4 different nodes. Among the 16 rows of one device no node is named by more than 8 rows, and in some devices' rows one node is named by exactly 8 rows. `expert_picks`: each row holds 8 different numbers; number p stands for local expert p % 2 of node node_lists[row, p // 2]. `cache_lengths`: the rows of every device include one of length 128.
All inputs are finite; a program needn't handle non-finite values.
Results may differ from the reference program's by a relative error of at most 0.005.
Values may be sent and summed in bfloat16 or wider, within the bound.
No kernel may reach another device: no remote copies, remote signals or barrier semaphores. Data moves between devices by JAX's collectives and lax.ppermute only.
A program may use at most 64 MiB of HBM per device.

```python
import math
import jax
import jax.numpy as jnp
import numpy as np
from jax import lax

D = 3584
HID = 1024
TOP = 8
NODES_TOP = 4
HEADS = 64
LAT = 512
ROPE = 64
ROWS = 16
ATT_ROWS = 8
CACHE = 128
EXPERTS = 16
EXP_NODE = 2
ROWS_ALL = 256
ATT_ALL = 128
CAP = 8
N_NODE = 8


def draw_query_latent(key, part):
    key = jax.random.fold_in(key, 3)
    values = jnp.clip(jax.random.normal(key, (ATT_ALL, HEADS, LAT), jnp.float32), -6.0, 6.0)
    return values.astype(jnp.bfloat16)


def draw_query_rope(key, part):
    key = jax.random.fold_in(key, 5)
    values = jnp.clip(jax.random.normal(key, (ATT_ALL, HEADS, ROPE), jnp.float32), -6.0, 6.0)
    return values.reshape(ATT_ALL, HEADS * ROPE).astype(jnp.bfloat16)


def draw_cache_rope(key, part):
    key = jax.random.fold_in(key, 7)
    values = jnp.clip(jax.random.normal(key, (ATT_ALL, ROPE, CACHE), jnp.float32), -6.0, 6.0)
    return values.astype(jnp.bfloat16)


def draw_expert_picks(key, part):
    key = jax.random.fold_in(key, 11)
    width_all = NODES_TOP * EXP_NODE
    raw_bits = jax.random.randint(key, (ROWS_ALL, width_all), 0, 2 ** 20, dtype=jnp.int32)
    distinct = raw_bits * width_all + jnp.arange(width_all, dtype=jnp.int32)[None, :]
    ordering = jnp.argsort(distinct, axis=1, stable=True)
    return ordering[:, :TOP].astype(jnp.int32)


def draw_cache_lengths(key, part):
    key = jax.random.fold_in(key, 13)
    key_first = jax.random.fold_in(key, 1)
    key_second = jax.random.fold_in(key, 2)
    lengths_base = jax.random.randint(key_first, (ATT_ALL,), 2, CACHE + 1, dtype=jnp.int32)
    long_row = jax.random.randint(key_second, (ATT_ALL // ATT_ROWS,), 0, ATT_ROWS, dtype=jnp.int32)
    row_index = jnp.arange(ATT_ALL, dtype=jnp.int32)
    is_long = row_index % ATT_ROWS == long_row[row_index // ATT_ROWS]
    return jnp.where(is_long, CACHE, lengths_base).astype(jnp.int32)


def shard_levels(own_key, extent, cuts, least, top_value):
    def one(axis_at, parts):
        draws = jax.random.uniform(jax.random.fold_in(jax.random.fold_in(own_key, 6), axis_at), (parts,), jnp.float32, least / len(cuts), top_value / len(cuts))
        return jnp.repeat(jnp.exp(draws), extent[axis_at] // parts).reshape((-1,) + (1,) * (len(extent) - axis_at - 1))

    level = one(*cuts[0])
    for cut in cuts[1:]:
        level = level * one(*cut)
    return level


def routed_block(own_key, own, number, rows, count, top, bound, slope):
    ranking = jax.random.permutation(own_key, count)
    packed, ordinary = load_shares(count, rows * top, bound, slope, True), load_shares(count, rows * top, bound, slope, False)
    places = jnp.arange(count)

    def named(sizes, offset_by):
        used = int((sizes > 0).sum())
        fixed = max(1, used // 4)
        passed = fixed + (places - fixed + offset_by * (used - fixed)) % max(1, count - fixed)
        return jnp.zeros((count,), jnp.int32).at[ranking[jnp.where(places < fixed, places, passed)]].set(jnp.asarray(sizes, jnp.int32))

    sizes = jnp.where(number % 4 == 0, named(packed, number // 4), named(ordinary, number - number // 4 - 1))
    mixed = jax.random.permutation(jax.random.fold_in(own, 3), count)
    donor, sink = mixed[0:count // 2 * 2:2], mixed[1:count // 2 * 2:2]
    margin = jnp.minimum(sizes[donor] - 1, bound - sizes[sink]) // 2
    margin = jnp.where((donor == ranking[0]) | (sink == ranking[0]) | (sizes[sink] == 0), 0, jnp.maximum(margin, 0))
    passed = jax.random.randint(jax.random.fold_in(own, 4), (count // 2,), 0, 1 << 20) % (margin + 1)
    sizes = sizes.at[donor].add(-passed).at[sink].add(passed)
    members = jnp.searchsorted(jnp.cumsum(sizes), jnp.arange(rows * top), side="right").astype(jnp.int32)
    listing = members.reshape(top, rows).T
    listing = listing[jax.random.permutation(jax.random.fold_in(own, 1), rows)]
    offset_by = jax.random.randint(jax.random.fold_in(own, 2), (rows, 1), 0, top)
    return jnp.take_along_axis(listing, (jnp.arange(top)[None, :] + offset_by) % top, axis=1)


def load_shares(number_of, total, limit, skew, full):
    loads = [(1 << 20) // math.isqrt(grade ** skew) + 1 for grade in range(1, number_of + 1)]
    largest = limit if full else min(limit, max(-(-total // number_of), total * loads[0] // sum(loads)))
    least = 1 if total - largest >= number_of - 1 else 0
    given, surplus = [largest] + [least] * (number_of - 1), total - largest - least * (number_of - 1)
    while surplus > 0:
        candidates = [i for i in range(1, number_of) if given[i] < largest] or [i for i in range(1, number_of) if given[i] < limit]
        mass, remaining = sum([loads[i] for i in candidates]), surplus
        for i in candidates:
            extra = min(limit - given[i], max(1, remaining * loads[i] // mass), surplus)
            given[i] = given[i] + extra
            surplus = surplus - extra
    return np.array(given)


def scatter_about(key, extent, spread, limit, shards=(), kind=jnp.bfloat16):
    loudness = shard_levels(key, extent, shards, -0.22, 0.18) if shards else 1.0
    values = jax.random.normal(key, extent, jnp.float32) * spread * loudness
    return jnp.minimum(jnp.maximum(values, -limit), limit).astype(kind)


def setup_inputs(seed: int = 0, part: int = 0) -> dict:
    streams_of = jax.random.split(jax.random.key(seed), 11)
    part_splits = jax.random.split(jax.random.fold_in(streams_of[10], part), 11)
    expert_hidden = scatter_about(part_splits[0], (ROWS_ALL, TOP, HID), 1.0, 6.0, ((0, 16),))
    gate_scores = jnp.clip(jnp.exp(math.log(1.0) - 2.9957323 * jax.random.uniform(part_splits[1], (ROWS_ALL, TOP), jnp.float32) ** shard_levels(part_splits[1], (ROWS_ALL, TOP), ((0, 16),), -0.2, 0.2)), 0.05, 1.0)
    node_lists_keys = jax.random.split(jax.random.fold_in(part_splits[2], 1), ROWS_ALL // ROWS)
    node_lists_turns = jax.random.permutation(jax.random.fold_in(part_splits[2], 3), ROWS_ALL // ROWS)
    node_lists = jax.vmap(lambda own, number: routed_block(jax.random.fold_in(part_splits[2], 2), own, number, ROWS, N_NODE, NODES_TOP, CAP, 2))(node_lists_keys, node_lists_turns).reshape((ROWS_ALL, NODES_TOP))
    expert_picks = draw_expert_picks(jax.random.fold_in(jax.random.fold_in(streams_of[10], part), 71), part)
    routed_down = scatter_about(streams_of[4], (EXPERTS, HID, D), HID ** -0.5, 0.1875, ((0, 16),))
    query_latent = draw_query_latent(jax.random.fold_in(jax.random.fold_in(streams_of[10], part), 71), part)
    query_rope = draw_query_rope(jax.random.fold_in(jax.random.fold_in(streams_of[10], part), 71), part)
    cache_latent = scatter_about(part_splits[7], (ATT_ALL, CACHE, LAT), 1.0, 6.0, ((0, 16),))
    cache_rope = draw_cache_rope(jax.random.fold_in(jax.random.fold_in(streams_of[10], part), 71), part)
    cache_lengths = draw_cache_lengths(jax.random.fold_in(jax.random.fold_in(streams_of[10], part), 71), part)
    return dict(expert_hidden=expert_hidden, gate_scores=gate_scores, node_lists=node_lists, expert_picks=expert_picks, routed_down=routed_down, query_latent=query_latent, query_rope=query_rope, cache_latent=cache_latent, cache_rope=cache_rope, cache_lengths=cache_lengths)


score_scale = 192.0 ** -0.5
route_scale = 2.5


def attend_block(pieces):
    query_latent, query_rope, cache_latent, cache_rope, cache_lengths = pieces
    row_count = query_latent.shape[0]
    latent_term = jnp.einsum("rhl,rcl->rhc", query_latent.astype(jnp.float32), cache_latent.astype(jnp.float32))
    rope_query = query_rope.reshape(row_count, HEADS, ROPE).astype(jnp.float32)
    rope_term = jnp.einsum("rhp,rpc->rhc", rope_query, cache_rope.astype(jnp.float32))
    scores = (latent_term + rope_term) * score_scale
    position = jnp.arange(CACHE, dtype=jnp.int32)
    valid = position[None, None, :] < cache_lengths[:, None, None]
    scores = jnp.where(valid, scores, -jnp.inf)
    highest = jnp.max(scores, axis=-1, keepdims=True)
    expd = jnp.exp(scores - highest)
    probs = (expd / jnp.sum(expd, axis=-1, keepdims=True)).astype(jnp.bfloat16)
    context = jnp.einsum("rhc,rcl->rhl", probs.astype(jnp.float32), cache_latent.astype(jnp.float32))
    return context.astype(jnp.bfloat16)


def reference(expert_hidden, gate_scores, node_lists, expert_picks, routed_down, query_latent, query_rope, cache_latent, cache_rope, cache_lengths):
    combine = (route_scale * gate_scores / jnp.sum(gate_scores, axis=-1, keepdims=True)).astype(jnp.bfloat16)
    node_index = (expert_picks // EXP_NODE).astype(jnp.int32)
    experts = (jnp.take_along_axis(node_lists, node_index, axis=1) * EXP_NODE + expert_picks % EXP_NODE).astype(jnp.int32)
    flat_experts = experts.reshape(-1)
    flat_hidden = expert_hidden.reshape(-1, HID)
    flat_weights = combine.reshape(-1).astype(jnp.float32)
    bucket = (ROWS_ALL // ROWS) * CAP
    slot_index = jnp.arange(bucket, dtype=jnp.int32)

    def one_expert(total, expert_id):
        hits = flat_experts == expert_id
        count = jnp.sum(hits.astype(jnp.int32))
        chosen = jnp.nonzero(hits, size=bucket, fill_value=0)[0].astype(jnp.int32)
        weights = jnp.where(slot_index < count, flat_weights[chosen], jnp.zeros((bucket,), jnp.float32))
        output = jnp.dot(flat_hidden[chosen], routed_down[expert_id], preferred_element_type=jnp.float32)
        total = total.at[chosen // TOP].add(output * weights[:, None])
        return total, None

    routed, unused = lax.scan(one_expert, jnp.zeros((ROWS_ALL, D), jnp.float32), jnp.arange(EXPERTS, dtype=jnp.int32))
    moe_out = routed.astype(jnp.bfloat16)
    blocks = ATT_ALL // ATT_ROWS
    context = lax.map(attend_block, (
        query_latent.reshape(blocks, ATT_ROWS, HEADS, LAT),
        query_rope.reshape(blocks, ATT_ROWS, HEADS * ROPE),
        cache_latent.reshape(blocks, ATT_ROWS, CACHE, LAT),
        cache_rope.reshape(blocks, ATT_ROWS, ROPE, CACHE),
        cache_lengths.reshape(blocks, ATT_ROWS)))
    return moe_out, context.reshape(ATT_ALL, HEADS, LAT)
```

```python
import functools

import jax
import jax.numpy as jnp
from jax import lax
from jax.experimental import pallas as pl
from jax.experimental.pallas import tpu as pltpu
from jax.sharding import PartitionSpec as P

NODES_TOP = 4


score_scale = 192.0 ** (-0.5)
route_scale = 2.5


def attend(query_latent, query_rope, cache_latent, cache_rope, cache_lengths):
    row_count, head_count, latent_width = query_latent.shape
    rope_width = cache_rope.shape[1]
    scores = jnp.einsum(
        "rhl,rcl->rhc", query_latent, cache_latent, preferred_element_type=jnp.float32
    )
    rope_query = query_rope.reshape(row_count, head_count, rope_width)
    scores = scores + jnp.einsum(
        "rhp,rpc->rhc", rope_query, cache_rope, preferred_element_type=jnp.float32
    )
    scores = scores * score_scale
    position = jnp.arange(cache_latent.shape[1], dtype=jnp.int32)
    valid = position[None, None, :] < cache_lengths[:, None, None]
    scores = jnp.where(valid, scores, -jnp.inf)
    highest = jnp.max(scores, axis=-1, keepdims=True)
    expd = jnp.exp(scores - highest)
    probs = (expd / jnp.sum(expd, axis=-1, keepdims=True)).astype(jnp.bfloat16)
    context = jnp.einsum("rhc,rcl->rhl", probs, cache_latent, preferred_element_type=jnp.float32)
    return context.astype(jnp.bfloat16)


def iota(shape, dim):
    return lax.broadcasted_iota(jnp.int32, shape, dim)


def pack_kernel(
    node_count, lane_count, capacity, scores_ref, lists_ref, picks_ref, hidden_ref, send_ref, place_ref
):
    pick_count, row_count = scores_ref.shape
    items = pick_count * row_count
    slots = node_count * capacity
    hidden_width = hidden_ref.shape[1]
    me = lax.axis_index("lane")

    def exact(a, b):
        return jnp.dot(a.astype(jnp.bfloat16), b.astype(jnp.bfloat16), preferred_element_type=jnp.float32)

    scores = scores_ref[...]
    combine = route_scale * scores / jnp.sum(scores, axis=0, keepdims=True)
    combine = combine.astype(jnp.bfloat16).astype(jnp.float32)
    picks = picks_ref[...]
    lists = lists_ref[...]
    choice = picks // lane_count
    lane = lax.rem(picks - choice * lane_count - me + lane_count, lane_count)
    node = jnp.zeros_like(picks)
    nodes = iota((node_count, row_count), 0)
    member = jnp.zeros((node_count, row_count), jnp.float32)
    for j in range(lists.shape[0]):
        node = jnp.where(choice == j, lists[j : j + 1, :], node)
        member = jnp.where(nodes == lists[j : j + 1, :], 1.0, member)
    before = iota((row_count, row_count), 0) < iota((row_count, row_count), 1)
    earlier = exact(member, jnp.where(before, 1.0, 0.0))

    spread = iota((row_count, items), 1) // pick_count == iota((row_count, items), 0)
    spread = jnp.where(spread, 1.0, 0.0)
    own_pick = lax.rem(iota((pick_count, items), 1), pick_count) == iota((pick_count, items), 0)

    def flat(values):
        wide = exact(values.astype(jnp.float32), spread)
        return jnp.sum(jnp.where(own_pick, wide, 0.0), axis=0, keepdims=True)

    weight = flat(combine)
    node_flat = flat(node).astype(jnp.int32)
    lane_flat = flat(lane).astype(jnp.int32)
    earlier_wide = exact(earlier, spread)
    named = iota((node_count, items), 0) == node_flat
    slot_flat = jnp.sum(jnp.where(named, earlier_wide, 0.0), axis=0, keepdims=True).astype(jnp.int32)
    target = node_flat * capacity + slot_flat
    at = iota((slots, items), 0) == target
    hidden = hidden_ref[...]
    for q in range(lane_count):
        placing = jnp.where(at & (lane_flat == q), weight, 0.0).astype(jnp.bfloat16)
        part = jnp.dot(placing, hidden, preferred_element_type=jnp.float32)
        send_ref[:, q * hidden_width : (q + 1) * hidden_width] = part.astype(jnp.bfloat16)

    slot_node = iota((slots, node_count), 0) // capacity == iota((slots, node_count), 1)
    marked = jnp.where(member > 0.0, earlier, -1.0)
    marked = exact(jnp.where(slot_node, 1.0, 0.0), marked)
    number = lax.rem(iota((slots, row_count), 0), capacity).astype(jnp.float32)
    place_ref[...] = jnp.where(marked == number, 1.0, 0.0).astype(jnp.bfloat16)


def expert_kernel(received_ref, *refs):
    *weight_refs, out_ref = refs
    depth = weight_refs[0].shape[0]
    total = None
    for q, weight_ref in enumerate(weight_refs):
        part = jnp.dot(
            received_ref[:, q * depth : (q + 1) * depth], weight_ref[...], preferred_element_type=jnp.float32
        )
        total = part if total is None else total + part
    out_ref[...] = total.astype(jnp.bfloat16)


def sum_kernel(place_ref, returned_ref, out_ref):
    total = lax.dot_general(
        place_ref[...], returned_ref[...], (((0,), (0,)), ((), ())), preferred_element_type=jnp.float32
    )
    out_ref[...] = total.astype(jnp.bfloat16)


def local(
    expert_hidden,
    gate_scores,
    node_lists,
    expert_picks,
    routed_down,
    query_latent,
    query_rope,
    cache_latent,
    cache_rope,
    cache_lengths,
):
    node_count = lax.axis_size("node")
    lane_count = lax.axis_size("lane")
    row_count, pick_count, hidden_width = expert_hidden.shape
    width = routed_down.shape[2]
    capacity = max(
        2, min(row_count // 2, 2 * ((row_count * NODES_TOP + node_count - 1) // node_count))
    )
    slots = node_count * capacity
    down_matrix = routed_down[0]
    matrices = [down_matrix]
    for q in range(1, lane_count):
        matrices.append(
            lax.ppermute(
                down_matrix, "lane", [((i + q) % lane_count, i) for i in range(lane_count)]
            )
        )
    send, place = pl.pallas_call(
        functools.partial(pack_kernel, node_count, lane_count, capacity),
        out_shape=(
            jax.ShapeDtypeStruct((slots, lane_count * hidden_width), jnp.bfloat16),
            jax.ShapeDtypeStruct((slots, row_count), jnp.bfloat16),
        ),
        name="pack",
    )(gate_scores.T, node_lists.T, expert_picks.T, expert_hidden.reshape(-1, hidden_width))
    received = lax.all_to_all(
        send.reshape(node_count, capacity, -1), "node", split_axis=0, concat_axis=0, tiled=True
    ).reshape(slots, -1)
    tile = 512
    output = pl.pallas_call(
        expert_kernel,
        grid=(width // tile,),
        in_specs=[pl.BlockSpec((slots, lane_count * hidden_width), lambda i: (0, 0))]
        + [pl.BlockSpec((hidden_width, tile), lambda i: (0, i))] * lane_count,
        out_specs=pl.BlockSpec((slots, tile), lambda i: (0, i)),
        out_shape=jax.ShapeDtypeStruct((slots, width), jnp.bfloat16),
        compiler_params=pltpu.CompilerParams(vmem_limit_bytes=24 * 2**20),
        name="experts",
    )(received, *matrices)
    returned = lax.all_to_all(
        output.reshape(node_count, capacity, width), "node", split_axis=0, concat_axis=0, tiled=True
    ).reshape(slots, width)
    moe_out = pl.pallas_call(
        sum_kernel,
        out_shape=jax.ShapeDtypeStruct((row_count, width), jnp.bfloat16),
        name="sum",
    )(place, returned)
    context = attend(query_latent, query_rope, cache_latent, cache_rope, cache_lengths)
    return (moe_out, context)


def solution(mesh):
    placed = (
        P(("groups", "node", "lane"), None, None),
        P(("groups", "node", "lane"), None),
        P(("groups", "node", "lane"), None),
        P(("groups", "node", "lane"), None),
        P(("node", "lane"), None, None),
        P(("groups", "node", "lane"), None, None),
        P(("groups", "node", "lane"), None),
        P(("groups", "node", "lane"), None, None),
        P(("groups", "node", "lane"), None, None),
        P(("groups", "node", "lane")),
    )
    return jax.shard_map(
        local,
        mesh=mesh,
        in_specs=placed,
        out_specs=(P(("groups", "node", "lane"), None), P(("groups", "node", "lane"), None, None)),
        check_vma=False,
    )
```

```python
import functools

import jax
import jax.numpy as jnp
from jax import lax
from jax.experimental import pallas as pl
from jax.experimental.pallas import tpu as pltpu
from jax.sharding import PartitionSpec as P

NODES_TOP = 4
MIB = 2**20


score_scale = 192.0 ** (-0.5)
route_scale = 2.5


def attend_kernel(lengths_ref, latent_ref, rope_ref, keys_ref, rope_keys_ref, out_ref):
    for row in range(latent_ref.shape[0]):
        keys = keys_ref[row]
        scores = lax.dot_general(
            latent_ref[row], keys, (((1,), (1,)), ((), ())), preferred_element_type=jnp.float32
        )
        scores = scores + jnp.dot(rope_ref[row], rope_keys_ref[row], preferred_element_type=jnp.float32)
        scores = scores * score_scale
        valid = iota(scores.shape, 1) < lengths_ref[row]
        scores = jnp.where(valid, scores, -jnp.inf)
        expd = jnp.exp(scores - jnp.max(scores, axis=-1, keepdims=True))
        probs = (expd / jnp.sum(expd, axis=-1, keepdims=True)).astype(jnp.bfloat16)
        context = jnp.dot(probs, keys, preferred_element_type=jnp.float32)
        out_ref[row] = context.astype(jnp.bfloat16)


def attend(query_latent, query_rope, cache_latent, cache_rope, cache_lengths):
    row_count, head_count, latent_width = query_latent.shape
    rope_width, position_count = cache_rope.shape[1:]
    rope_query = query_rope.reshape(row_count, head_count, rope_width)
    products = head_count * position_count * (2 * latent_width + rope_width)
    return pl.pallas_call(
        attend_kernel,
        in_specs=[pl.BlockSpec(memory_space=pltpu.SMEM)] + [pl.BlockSpec(memory_space=pltpu.VMEM)] * 4,
        out_specs=pl.BlockSpec(memory_space=pltpu.VMEM),
        out_shape=jax.ShapeDtypeStruct(query_latent.shape, jnp.bfloat16),
        compiler_params=pltpu.CompilerParams(vmem_limit_bytes=8 * MIB),
        cost_estimate=pl.CostEstimate(
            flops=2 * row_count * products,
            bytes_accessed=2 * (2 * query_latent.size + query_rope.size + cache_latent.size + cache_rope.size),
            transcendentals=row_count * head_count * position_count,
        ),
        name="attend",
    )(cache_lengths, query_latent, rope_query, cache_latent, cache_rope)


def iota(shape, dim):
    return lax.broadcasted_iota(jnp.int32, shape, dim)


def exact(a, b):
    return jnp.dot(a.astype(jnp.bfloat16), b.astype(jnp.bfloat16), preferred_element_type=jnp.float32)


def meeting(node_count, a, b):
    return a ^ b if node_count & (node_count - 1) == 0 else (a + b) % node_count


def partner(node_count, a, number):
    return a ^ number if node_count & (node_count - 1) == 0 else (number - a) % node_count


def turn_of(node_count, lane, number):
    late = node_count - 1 - number
    turn = late // 2
    return jnp.where(late % 2 == (lane + turn) % 2, turn, -1)


def number_of(node_count, lane, turn):
    return node_count - 1 - 2 * turn - (lane + turn) % 2


def pack_kernel(node_count, lane_count, capacity, *refs):
    sources = [refs[4 * s : 4 * s + 4] for s in range(lane_count)]
    send_refs = refs[4 * lane_count : -1]
    place_ref = refs[-1]
    pick_count, row_count = sources[0][0].shape
    items = pick_count * row_count
    block = lane_count * capacity
    slots = len(send_refs) * block
    hidden_width = sources[0][3].shape[1]
    lane_here = lax.axis_index("lane")
    node_here = lax.axis_index("node")

    spread = iota((row_count, items), 1) // pick_count == iota((row_count, items), 0)
    spread = jnp.where(spread, 1.0, 0.0).astype(jnp.bfloat16)
    own_pick = lax.rem(iota((pick_count, items), 1), pick_count) == iota((pick_count, items), 0)
    before = iota((row_count, row_count), 0) < iota((row_count, row_count), 1)
    before = jnp.where(before, 1.0, 0.0)
    nodes = iota((node_count, row_count), 0)
    places = iota((slots, items), 0)

    def flat(values):
        wide = exact(values, spread)
        return jnp.sum(jnp.where(own_pick, wide, 0.0), axis=0, keepdims=True)

    parts = [None] * lane_count
    for s, (scores_ref, lists_ref, picks_ref, hidden_ref) in enumerate(sources):
        scores = scores_ref[...]
        combine = (route_scale * scores / jnp.sum(scores, axis=0, keepdims=True)).astype(jnp.bfloat16)
        picks = picks_ref[...]
        lists = lists_ref[...]
        choice = picks // lane_count
        order = lax.rem(picks - choice * lane_count - lane_here + lane_count, lane_count)
        node = jnp.zeros_like(picks)
        member = jnp.zeros((node_count, row_count), jnp.float32)
        for j in range(lists.shape[0]):
            node = jnp.where(choice == j, lists[j : j + 1, :], node)
            member = jnp.where(nodes == lists[j : j + 1, :], 1.0, member)
        earlier = exact(exact(member, before), spread)
        weight = flat(combine)
        node_and_order = flat((node * lane_count + order).astype(jnp.float32)).astype(jnp.int32)
        node_flat = node_and_order // lane_count
        order_flat = node_and_order - node_flat * lane_count
        named = iota((node_count, items), 0) == node_flat
        slot = jnp.sum(jnp.where(named, earlier, 0.0), axis=0, keepdims=True).astype(jnp.int32)
        turn = turn_of(node_count, lane_here, meeting(node_count, node_here, node_flat))
        target = jnp.where(turn >= 0, (turn * lane_count + s) * capacity + slot, -1)
        at = places == target
        hidden = hidden_ref[...]
        for q in range(lane_count):
            placing = jnp.where(at & (order_flat == q), weight, 0.0).astype(jnp.bfloat16)
            part = jnp.dot(placing, hidden, preferred_element_type=jnp.float32)
            parts[q] = part if parts[q] is None else parts[q] + part
        marks = lax.dot_general(
            jnp.where(at, 1.0, 0.0).astype(jnp.bfloat16),
            spread,
            (((1,), (1,)), ((), ())),
            preferred_element_type=jnp.float32,
        )
        place_ref[:, s * row_count : (s + 1) * row_count] = jnp.where(marks > 0.0, 1.0, 0.0)
    for q in range(lane_count):
        columns = slice(q * hidden_width, (q + 1) * hidden_width)
        for turn, send_ref in enumerate(send_refs):
            send_ref[:, columns] = parts[q][turn * block : (turn + 1) * block].astype(jnp.bfloat16)


def fetch_kernel(matrix_ref, out_ref, sem):
    copy = pltpu.make_async_copy(matrix_ref, out_ref, sem)
    copy.start()
    copy.wait()


def expert_kernel(turns, tile, *refs):
    received_refs, refs = refs[:turns], refs[turns:]
    out_refs, refs = refs[-turns - 1 : -1], refs[: -turns - 1] + refs[-1:]
    *weight_refs, rows_ref = refs
    depth, width = weight_refs[0].shape
    block = received_refs[0].shape[0]
    for turn, received_ref in enumerate(received_refs):
        rows_ref[turn * block : (turn + 1) * block, :] = received_ref[...]

    @pl.loop(0, width // tile)
    def _(i):
        columns = pl.ds(pl.multiple_of(i * tile, tile), tile)
        total = None
        for q, weight_ref in enumerate(weight_refs):
            part = jnp.dot(
                rows_ref[:, q * depth : (q + 1) * depth],
                weight_ref[:, columns],
                preferred_element_type=jnp.float32,
            )
            total = part if total is None else total + part
        total = total.astype(jnp.bfloat16)
        for turn, out_ref in enumerate(out_refs):
            out_ref[:, columns] = total[turn * block : (turn + 1) * block]


def sum_kernel(place_ref, *refs):
    *returned_refs, own_ref, other_ref, all_ref = refs
    block = returned_refs[0].shape[0]
    rows = own_ref.shape[0]
    for turn, returned_ref in enumerate(returned_refs):
        all_ref[turn * block : (turn + 1) * block, :] = returned_ref[...]
    total = lax.dot_general(
        place_ref[...].astype(jnp.bfloat16),
        all_ref[...],
        (((0,), (0,)), ((), ())),
        preferred_element_type=jnp.float32,
    )
    own_ref[...] = total[:rows]
    other_ref[...] = total[rows:]


def local(
    expert_hidden,
    gate_scores,
    node_lists,
    expert_picks,
    routed_down,
    query_latent,
    query_rope,
    cache_latent,
    cache_rope,
    cache_lengths,
):
    node_count = lax.axis_size("node")
    lane_count = lax.axis_size("lane")
    row_count, pick_count, hidden_width = expert_hidden.shape
    width = routed_down.shape[2]
    capacity = max(
        2, min(row_count // 2, 2 * ((row_count * NODES_TOP + node_count - 1) // node_count))
    )
    turns = node_count // lane_count
    block = lane_count * capacity
    slots = turns * block

    def other_core(value):
        return lax.ppermute(value, "lane", [(0, 1), (1, 0)])

    def meet(values):
        out = []
        for turn, value in enumerate(values):
            pairs = []
            for node in range(node_count):
                for lane in range(lane_count):
                    there = partner(node_count, node, number_of(node_count, lane, turn))
                    pairs.append((node * lane_count + lane, there * lane_count + lane))
            out.append(lax.ppermute(value, ("node", "lane"), pairs))
        return out

    mine = [gate_scores.T, node_lists.T, expert_picks.T, expert_hidden.reshape(-1, hidden_width)]
    theirs = [other_core(value) for value in mine]
    down_matrix, *theirs = lax.optimization_barrier((routed_down[0], *theirs))
    other_matrix = other_core(down_matrix)
    *send, place = pl.pallas_call(
        functools.partial(pack_kernel, node_count, lane_count, capacity),
        out_shape=[jax.ShapeDtypeStruct((block, lane_count * hidden_width), jnp.bfloat16)] * turns
        + [jax.ShapeDtypeStruct((slots, lane_count * row_count), jnp.float32)],
        compiler_params=pltpu.CompilerParams(vmem_limit_bytes=8 * MIB),
        name="pack",
    )(*[pltpu.with_memory_space_constraint(value, pltpu.HBM) for value in mine], *theirs)
    received = meet(send)
    whole = pl.BlockSpec(memory_space=pltpu.VMEM)
    down_matrix, _ = lax.optimization_barrier((down_matrix, place))
    own_matrix = pl.pallas_call(
        fetch_kernel,
        in_specs=[pl.BlockSpec(memory_space=pltpu.HBM)],
        out_specs=whole,
        out_shape=pltpu.VMEM(down_matrix.shape, down_matrix.dtype),
        scratch_shapes=[pltpu.SemaphoreType.DMA],
        compiler_params=pltpu.CompilerParams(vmem_limit_bytes=MIB),
        cost_estimate=pl.CostEstimate(flops=0, bytes_accessed=4 * down_matrix.size, transcendentals=0),
        name="fetch",
    )(pltpu.with_memory_space_constraint(down_matrix, pltpu.HBM))
    output = pl.pallas_call(
        functools.partial(expert_kernel, turns, 512),
        in_specs=[whole] * (turns + lane_count),
        out_specs=[whole] * turns,
        out_shape=[jax.ShapeDtypeStruct((block, width), jnp.bfloat16)] * turns,
        scratch_shapes=[pltpu.VMEM((slots, lane_count * hidden_width), jnp.bfloat16)],
        compiler_params=pltpu.CompilerParams(vmem_limit_bytes=24 * MIB),
        name="experts",
    )(*received, *[pltpu.with_memory_space_constraint(m, pltpu.VMEM) for m in (own_matrix, other_matrix)])
    returned = meet(output)
    query_latent, query_rope, cache_latent, cache_rope, cache_lengths, _ = lax.optimization_barrier(
        (query_latent, query_rope, cache_latent, cache_rope, cache_lengths, output[0])
    )
    context = attend(query_latent, query_rope, cache_latent, cache_rope, cache_lengths)
    *returned, context = lax.optimization_barrier((*returned, context))
    own, other = pl.pallas_call(
        sum_kernel,
        out_shape=[jax.ShapeDtypeStruct((row_count, width), jnp.float32)] * 2,
        scratch_shapes=[pltpu.VMEM((slots, width), jnp.bfloat16)],
        compiler_params=pltpu.CompilerParams(vmem_limit_bytes=8 * MIB),
        name="sum",
    )(place, *returned)
    moe_out = (own + other_core(other)).astype(jnp.bfloat16)
    return (moe_out, context)


def solution(mesh):
    placed = (
        P(("groups", "node", "lane"), None, None),
        P(("groups", "node", "lane"), None),
        P(("groups", "node", "lane"), None),
        P(("groups", "node", "lane"), None),
        P(("node", "lane"), None, None),
        P(("groups", "node", "lane"), None, None),
        P(("groups", "node", "lane"), None),
        P(("groups", "node", "lane"), None, None),
        P(("groups", "node", "lane"), None, None),
        P(("groups", "node", "lane")),
    )
    return jax.shard_map(
        local,
        mesh=mesh,
        in_specs=placed,
        out_specs=(P(("groups", "node", "lane"), None), P(("groups", "node", "lane"), None, None)),
        check_vma=False,
    )
```

```python
import functools

import jax
import jax.numpy as jnp
from jax import lax
from jax.experimental import pallas as pl
from jax.experimental.pallas import tpu as pltpu
from jax.sharding import PartitionSpec as P

NODES_TOP = 4
MIB = 2**20
TILE = 512


score_scale = 192.0 ** (-0.5)
route_scale = 2.5


def attend_kernel(lengths_ref, latent_ref, rope_ref, keys_ref, rope_keys_ref, out_ref):
    row_count, head_count, _ = latent_ref.shape
    scores = []
    for row in range(row_count):
        score = lax.dot_general(
            latent_ref[row], keys_ref[row], (((1,), (1,)), ((), ())), preferred_element_type=jnp.float32
        )
        score = score + jnp.dot(rope_ref[row], rope_keys_ref[row], preferred_element_type=jnp.float32)
        valid = iota(score.shape, 1) < lengths_ref[row]
        scores.append(jnp.where(valid, score * score_scale, -jnp.inf))
    scores = jnp.concatenate(scores, axis=0)
    expd = jnp.exp(scores - jnp.max(scores, axis=-1, keepdims=True))
    probs = (expd / jnp.sum(expd, axis=-1, keepdims=True)).astype(jnp.bfloat16)
    for row in range(row_count):
        context = jnp.dot(
            probs[row * head_count : (row + 1) * head_count], keys_ref[row], preferred_element_type=jnp.float32
        )
        out_ref[row] = context.astype(jnp.bfloat16)


def attend(query_latent, query_rope, cache_latent, cache_rope, cache_lengths):
    row_count, head_count, latent_width = query_latent.shape
    rope_width, position_count = cache_rope.shape[1:]
    rope_query = query_rope.reshape(row_count, head_count, rope_width)
    products = head_count * position_count * (2 * latent_width + rope_width)
    return pl.pallas_call(
        attend_kernel,
        in_specs=[pl.BlockSpec(memory_space=pltpu.SMEM)] + [pl.BlockSpec(memory_space=pltpu.VMEM)] * 4,
        out_specs=pl.BlockSpec(memory_space=pltpu.VMEM),
        out_shape=jax.ShapeDtypeStruct(query_latent.shape, jnp.bfloat16),
        compiler_params=pltpu.CompilerParams(vmem_limit_bytes=8 * MIB),
        cost_estimate=pl.CostEstimate(
            flops=2 * row_count * products,
            bytes_accessed=2 * (2 * query_latent.size + query_rope.size + cache_latent.size + cache_rope.size),
            transcendentals=row_count * head_count * position_count,
        ),
        name="attend",
    )(cache_lengths, query_latent, rope_query, cache_latent, cache_rope)


def iota(shape, dim):
    return lax.broadcasted_iota(jnp.int32, shape, dim)


def exact(a, b):
    return jnp.dot(a.astype(jnp.bfloat16), b.astype(jnp.bfloat16), preferred_element_type=jnp.float32)


def meeting(node_count, a, b):
    return a ^ b if node_count & (node_count - 1) == 0 else (a + b) % node_count


def partner(node_count, a, number):
    return a ^ number if node_count & (node_count - 1) == 0 else (number - a) % node_count


def turn_of(node_count, lane_count, lane, number):
    return jnp.where(number % lane_count == lane, (node_count - 1 - number) // lane_count, -1)


def number_of(node_count, lane_count, lane, turn):
    return node_count - lane_count * (turn + 1) + lane


def load_kernel(*refs):
    *refs, sems = refs
    half = len(refs) // 2
    copies = [
        pltpu.make_async_copy(in_ref, out_ref, sems.at[i])
        for i, (in_ref, out_ref) in enumerate(zip(refs[:half], refs[half:]))
    ]
    for copy in copies:
        copy.start()
    for copy in copies:
        copy.wait()


def pack_kernel(node_count, lane_count, capacity, *refs):
    sources = [refs[4 * s : 4 * s + 4] for s in range(lane_count)]
    send_refs = refs[4 * lane_count : -1]
    place_ref = refs[-1]
    pick_count, row_count = sources[0][0].shape
    items = pick_count * row_count
    block = lane_count * capacity
    slots = len(send_refs) * block
    hidden_width = sources[0][3].shape[1]
    lane_here = lax.axis_index("lane")
    node_here = lax.axis_index("node")

    spread = iota((row_count, items), 1) // pick_count == iota((row_count, items), 0)
    spread = jnp.where(spread, 1.0, 0.0).astype(jnp.bfloat16)
    own_pick = lax.rem(iota((pick_count, items), 1), pick_count) == iota((pick_count, items), 0)
    before = iota((row_count, row_count), 0) < iota((row_count, row_count), 1)
    before = jnp.where(before, 1.0, 0.0)
    nodes = iota((node_count, row_count), 0)
    places = iota((slots, items), 0)

    def flat(values):
        wide = exact(values, spread)
        return jnp.sum(jnp.where(own_pick, wide, 0.0), axis=0, keepdims=True)

    parts = [None] * lane_count
    for s, (scores_ref, lists_ref, picks_ref, hidden_ref) in enumerate(sources):
        scores = scores_ref[...]
        combine = (route_scale * scores / jnp.sum(scores, axis=0, keepdims=True)).astype(jnp.bfloat16)
        picks = picks_ref[...]
        lists = lists_ref[...]
        choice = picks // lane_count
        order = lax.rem(picks - choice * lane_count - lane_here + lane_count, lane_count)
        node = jnp.zeros_like(picks)
        member = jnp.zeros((node_count, row_count), jnp.float32)
        for j in range(lists.shape[0]):
            node = jnp.where(choice == j, lists[j : j + 1, :], node)
            member = jnp.where(nodes == lists[j : j + 1, :], 1.0, member)
        earlier = exact(exact(member, before), spread)
        weight = flat(combine)
        node_and_order = flat((node * lane_count + order).astype(jnp.float32)).astype(jnp.int32)
        node_flat = node_and_order // lane_count
        order_flat = node_and_order - node_flat * lane_count
        named = iota((node_count, items), 0) == node_flat
        slot = jnp.sum(jnp.where(named, earlier, 0.0), axis=0, keepdims=True).astype(jnp.int32)
        turn = turn_of(node_count, lane_count, lane_here, meeting(node_count, node_here, node_flat))
        target = jnp.where(turn >= 0, (turn * lane_count + s) * capacity + slot, -1)
        at = places == target
        hidden = hidden_ref[...]
        for q in range(lane_count):
            placing = jnp.where(at & (order_flat == q), weight, 0.0).astype(jnp.bfloat16)
            part = jnp.dot(placing, hidden, preferred_element_type=jnp.float32)
            parts[q] = part if parts[q] is None else parts[q] + part
        marks = lax.dot_general(
            jnp.where(at, 1.0, 0.0).astype(jnp.bfloat16),
            spread,
            (((1,), (1,)), ((), ())),
            preferred_element_type=jnp.float32,
        )
        place_ref[:, s * row_count : (s + 1) * row_count] = jnp.where(marks > 0.0, 1.0, 0.0)
    for q in range(lane_count):
        columns = slice(q * hidden_width, (q + 1) * hidden_width)
        for turn, send_ref in enumerate(send_refs):
            send_ref[:, columns] = parts[q][turn * block : (turn + 1) * block].astype(jnp.bfloat16)


def fetch_kernel(matrix_ref, out_ref, sem):
    copy = pltpu.make_async_copy(matrix_ref.at[pl.ds(0, out_ref.shape[0])], out_ref, sem)
    copy.start()
    copy.wait()


def own_kernel(*refs):
    *received_refs, first_ref, matrix_ref, out_ref, second_ref, sem = refs
    depth, width = matrix_ref.shape
    head = first_ref.shape[0]
    copy = pltpu.make_async_copy(matrix_ref.at[pl.ds(head, depth - head)], second_ref, sem)
    copy.start()
    rows = jnp.concatenate([received_ref[:, :depth] for received_ref in received_refs], axis=0)
    for start in range(0, width, TILE):
        columns = slice(start, start + TILE)
        out_ref[:, columns] = jnp.dot(
            rows[:, :head], first_ref[:, columns], preferred_element_type=jnp.float32
        )
    copy.wait()
    for start in range(0, width, TILE):
        columns = slice(start, start + TILE)
        out_ref[:, columns] += jnp.dot(
            rows[:, head:], second_ref[:, columns], preferred_element_type=jnp.float32
        )


def other_kernel(turns, *refs):
    received_refs = refs[:turns]
    own_ref, weight_ref, *out_refs = refs[turns:]
    depth, width = weight_ref.shape
    block = received_refs[0].shape[0]
    rows = jnp.concatenate([received_ref[:, depth:] for received_ref in received_refs], axis=0)

    for start in range(0, width, TILE):
        columns = slice(start, start + TILE)
        part = jnp.dot(rows, weight_ref[:, columns], preferred_element_type=jnp.float32)
        total = (own_ref[:, columns] + part).astype(jnp.bfloat16)
        for turn, out_ref in enumerate(out_refs):
            out_ref[:, columns] = total[turn * block : (turn + 1) * block]


def sum_kernel(place_ref, *refs):
    *returned_refs, own_ref, other_ref, all_ref = refs
    block = returned_refs[0].shape[0]
    rows = own_ref.shape[0]
    for turn, returned_ref in enumerate(returned_refs):
        all_ref[turn * block : (turn + 1) * block, :] = returned_ref[...]
    total = lax.dot_general(
        place_ref[...].astype(jnp.bfloat16),
        all_ref[...],
        (((0,), (0,)), ((), ())),
        preferred_element_type=jnp.float32,
    )
    own_ref[...] = total[:rows]
    other_ref[...] = total[rows:]


def local(
    expert_hidden,
    gate_scores,
    node_lists,
    expert_picks,
    routed_down,
    query_latent,
    query_rope,
    cache_latent,
    cache_rope,
    cache_lengths,
):
    node_count = lax.axis_size("node")
    lane_count = lax.axis_size("lane")
    row_count, _, hidden_width = expert_hidden.shape
    width = routed_down.shape[2]
    capacity = max(
        2, min(row_count // 2, 2 * ((row_count * NODES_TOP + node_count - 1) // node_count))
    )
    turns = node_count // lane_count
    block = lane_count * capacity
    slots = turns * block

    def other_core(value):
        return lax.ppermute(value, "lane", [(0, 1), (1, 0)])

    def meet(values):
        out = []
        for turn, value in enumerate(values):
            pairs = []
            for node in range(node_count):
                for lane in range(lane_count):
                    there = partner(node_count, node, number_of(node_count, lane_count, lane, turn))
                    pairs.append((node * lane_count + lane, there * lane_count + lane))
            out.append(lax.ppermute(value, ("node", "lane"), pairs))
        return out

    whole = pl.BlockSpec(memory_space=pltpu.VMEM)
    outside = pl.BlockSpec(memory_space=pltpu.HBM)

    def in_hbm(value):
        return pltpu.with_memory_space_constraint(value, pltpu.HBM)

    def in_vmem(value):
        return pltpu.with_memory_space_constraint(value, pltpu.VMEM)

    def params(mib):
        return pltpu.CompilerParams(vmem_limit_bytes=mib * MIB)

    own_matrix = routed_down[0]
    mine = [gate_scores.T, node_lists.T, expert_picks.T, expert_hidden.reshape(-1, hidden_width)]
    theirs = [other_core(value) for value in mine]
    mine = pl.pallas_call(
        load_kernel,
        in_specs=[outside] * 4,
        out_specs=[whole] * 4,
        out_shape=[pltpu.VMEM(value.shape, value.dtype) for value in mine],
        scratch_shapes=[pltpu.SemaphoreType.DMA((4,))],
        compiler_params=params(1),
        name="load",
    )(*[in_hbm(value) for value in mine])
    sent_matrix, *_ = lax.optimization_barrier((own_matrix, *theirs, mine[0]))
    other_matrix = other_core(sent_matrix)
    *send, place = pl.pallas_call(
        functools.partial(pack_kernel, node_count, lane_count, capacity),
        in_specs=[whole] * 8,
        out_specs=[whole] * (turns + 1),
        out_shape=[jax.ShapeDtypeStruct((block, lane_count * hidden_width), jnp.bfloat16)] * turns
        + [jax.ShapeDtypeStruct((slots, lane_count * row_count), jnp.float32)],
        compiler_params=params(4),
        name="pack",
    )(*[in_vmem(value) for value in (*mine, *theirs)])
    received = meet(send)
    own_matrix, _ = lax.optimization_barrier((own_matrix, place))
    head = hidden_width * 3 // 4
    first = pl.pallas_call(
        fetch_kernel,
        in_specs=[outside],
        out_specs=whole,
        out_shape=pltpu.VMEM((head, width), own_matrix.dtype),
        scratch_shapes=[pltpu.SemaphoreType.DMA],
        compiler_params=params(1),
        cost_estimate=pl.CostEstimate(flops=0, bytes_accessed=4 * head * width, transcendentals=0),
        name="fetch",
    )(in_hbm(own_matrix))
    own_part = pl.pallas_call(
        own_kernel,
        in_specs=[whole] * (turns + 1) + [outside],
        out_specs=whole,
        out_shape=jax.ShapeDtypeStruct((slots, width), jnp.float32),
        scratch_shapes=[
            pltpu.VMEM((hidden_width - head, width), own_matrix.dtype),
            pltpu.SemaphoreType.DMA,
        ],
        compiler_params=params(8),
        name="own",
    )(*received, in_vmem(first), in_hbm(own_matrix))
    output = pl.pallas_call(
        functools.partial(other_kernel, turns),
        in_specs=[whole] * (turns + 2),
        out_specs=[whole] * turns,
        out_shape=[jax.ShapeDtypeStruct((block, width), jnp.bfloat16)] * turns,
        compiler_params=params(2),
        name="other",
    )(*received, in_vmem(own_part), in_vmem(other_matrix))
    returned = meet(output)
    query_latent, query_rope, cache_latent, cache_rope, cache_lengths, _ = lax.optimization_barrier(
        (query_latent, query_rope, cache_latent, cache_rope, cache_lengths, output[-1])
    )
    context = attend(query_latent, query_rope, cache_latent, cache_rope, cache_lengths)
    *returned, context = lax.optimization_barrier((*returned, context))
    own, other = pl.pallas_call(
        sum_kernel,
        out_shape=[jax.ShapeDtypeStruct((row_count, width), jnp.float32)] * 2,
        scratch_shapes=[pltpu.VMEM((slots, width), jnp.bfloat16)],
        compiler_params=pltpu.CompilerParams(vmem_limit_bytes=8 * MIB),
        name="sum",
    )(place, *returned)
    moe_out = (own + other_core(other)).astype(jnp.bfloat16)
    return (moe_out, context)


def solution(mesh):
    placed = (
        P(("groups", "node", "lane"), None, None),
        P(("groups", "node", "lane"), None),
        P(("groups", "node", "lane"), None),
        P(("groups", "node", "lane"), None),
        P(("node", "lane"), None, None),
        P(("groups", "node", "lane"), None, None),
        P(("groups", "node", "lane"), None),
        P(("groups", "node", "lane"), None, None),
        P(("groups", "node", "lane"), None, None),
        P(("groups", "node", "lane")),
    )
    return jax.shard_map(
        local,
        mesh=mesh,
        in_specs=placed,
        out_specs=(P(("groups", "node", "lane"), None), P(("groups", "node", "lane"), None, None)),
        check_vma=False,
    )
```

```python
import functools

import jax
import jax.numpy as jnp
from jax import lax
from jax.experimental import pallas as pl
from jax.experimental.pallas import tpu as pltpu
from jax.sharding import PartitionSpec as P

NODES_TOP = 4
MIB = 2**20
TILE = 512


score_scale = 192.0 ** (-0.5)
route_scale = 2.5


def attend_kernel(lengths_ref, latent_ref, rope_ref, keys_ref, rope_keys_ref, out_ref):
    row_count, head_count, _ = latent_ref.shape
    scores = []
    for row in range(row_count):
        score = lax.dot_general(
            latent_ref[row], keys_ref[row], (((1,), (1,)), ((), ())), preferred_element_type=jnp.float32
        )
        score = score + jnp.dot(rope_ref[row], rope_keys_ref[row], preferred_element_type=jnp.float32)
        valid = iota(score.shape, 1) < lengths_ref[row]
        scores.append(jnp.where(valid, score * score_scale, -jnp.inf))
    scores = jnp.concatenate(scores, axis=0)
    expd = jnp.exp(scores - jnp.max(scores, axis=-1, keepdims=True))
    probs = (expd / jnp.sum(expd, axis=-1, keepdims=True)).astype(jnp.bfloat16)
    for row in range(row_count):
        context = jnp.dot(
            probs[row * head_count : (row + 1) * head_count], keys_ref[row], preferred_element_type=jnp.float32
        )
        out_ref[row] = context.astype(jnp.bfloat16)


def attend(query_latent, query_rope, cache_latent, cache_rope, cache_lengths):
    row_count, head_count, latent_width = query_latent.shape
    rope_width, position_count = cache_rope.shape[1:]
    rope_query = query_rope.reshape(row_count, head_count, rope_width)
    products = head_count * position_count * (2 * latent_width + rope_width)
    return pl.pallas_call(
        attend_kernel,
        in_specs=[pl.BlockSpec(memory_space=pltpu.SMEM)] + [pl.BlockSpec(memory_space=pltpu.VMEM)] * 4,
        out_specs=pl.BlockSpec(memory_space=pltpu.VMEM),
        out_shape=jax.ShapeDtypeStruct(query_latent.shape, jnp.bfloat16),
        compiler_params=pltpu.CompilerParams(vmem_limit_bytes=8 * MIB),
        cost_estimate=pl.CostEstimate(flops=0, bytes_accessed=0, transcendentals=0),
        name="attend",
    )(cache_lengths, query_latent, rope_query, cache_latent, cache_rope)


def iota(shape, dim):
    return lax.broadcasted_iota(jnp.int32, shape, dim)


def exact(a, b):
    return jnp.dot(a.astype(jnp.bfloat16), b.astype(jnp.bfloat16), preferred_element_type=jnp.float32)


def meeting(node_count, a, b):
    return a ^ b if node_count & (node_count - 1) == 0 else (a + b) % node_count


def partner(node_count, a, number):
    return a ^ number if node_count & (node_count - 1) == 0 else (number - a) % node_count


def turn_of(node_count, lane_count, lane, number):
    return jnp.where(number % lane_count == lane, (node_count - 1 - number) // lane_count, -1)


def number_of(node_count, lane_count, lane, turn):
    return node_count - lane_count * (turn + 1) + lane


def load_kernel(*refs):
    *refs, sems = refs
    half = len(refs) // 2
    copies = [
        pltpu.make_async_copy(in_ref, out_ref, sems.at[i])
        for i, (in_ref, out_ref) in enumerate(zip(refs[:half], refs[half:]))
    ]
    for copy in copies:
        copy.start()
    for copy in copies:
        copy.wait()


def spread_of(pick_count, row_count):
    items = pick_count * row_count
    spread = iota((row_count, items), 1) // pick_count == iota((row_count, items), 0)
    return jnp.where(spread, 1.0, 0.0).astype(jnp.bfloat16)


def flat(values, spread):
    pick_count, _ = values.shape
    _, items = spread.shape
    own_pick = lax.rem(iota((pick_count, items), 1), pick_count) == iota((pick_count, items), 0)
    return jnp.sum(jnp.where(own_pick, exact(values, spread), 0.0), axis=0, keepdims=True)


def route(node_count, lane_count, lists, picks, spread):
    _, row_count = picks.shape
    _, items = spread.shape
    lane_here = lax.axis_index("lane")
    before = iota((row_count, row_count), 0) < iota((row_count, row_count), 1)
    nodes = iota((node_count, row_count), 0)
    choice = picks // lane_count
    order = lax.rem(picks - choice * lane_count - lane_here + lane_count, lane_count)
    node = jnp.zeros_like(picks)
    member = jnp.zeros((node_count, row_count), jnp.float32)
    for j in range(lists.shape[0]):
        node = jnp.where(choice == j, lists[j : j + 1, :], node)
        member = jnp.where(nodes == lists[j : j + 1, :], 1.0, member)
    earlier = exact(exact(member, jnp.where(before, 1.0, 0.0)), spread)
    both = flat((node * lane_count + order).astype(jnp.float32), spread).astype(jnp.int32)
    node = both // lane_count
    order = both - node * lane_count
    named = iota((node_count, items), 0) == node
    slot = jnp.sum(jnp.where(named, earlier, 0.0), axis=0, keepdims=True).astype(jnp.int32)
    return meeting(node_count, lax.axis_index("node"), node), slot, order


def target_of(node_count, lane_count, capacity, source, number, slot):
    turn = turn_of(node_count, lane_count, lax.axis_index("lane"), number)
    return jnp.where(turn >= 0, (turn * lane_count + source) * capacity + slot, -1)


def pack_kernel(node_count, lane_count, capacity, *refs):
    sources = [refs[4 * s : 4 * s + 4] for s in range(lane_count)]
    send_refs = refs[4 * lane_count :]
    block = lane_count * capacity
    slots = len(send_refs) * block
    hidden_width = sources[0][3].shape[1]
    spread = spread_of(*sources[0][0].shape)
    places = iota((slots, spread.shape[1]), 0)
    parts = [None] * lane_count
    for s, (scores_ref, lists_ref, picks_ref, hidden_ref) in enumerate(sources):
        scores = scores_ref[...]
        combine = (route_scale * scores / jnp.sum(scores, axis=0, keepdims=True)).astype(jnp.bfloat16)
        weight = flat(combine, spread)
        number, slot, order = route(node_count, lane_count, lists_ref[...], picks_ref[...], spread)
        at = places == target_of(node_count, lane_count, capacity, s, number, slot)
        hidden = hidden_ref[...]
        for q in range(lane_count):
            placing = jnp.where(at & (order == q), weight, 0.0).astype(jnp.bfloat16)
            part = jnp.dot(placing, hidden, preferred_element_type=jnp.float32)
            parts[q] = part if parts[q] is None else parts[q] + part
    for q in range(lane_count):
        columns = slice(q * hidden_width, (q + 1) * hidden_width)
        for turn, send_ref in enumerate(send_refs):
            send_ref[:, columns] = parts[q][turn * block : (turn + 1) * block].astype(jnp.bfloat16)


def fetch_kernel(node_count, lane_count, capacity, split, matrix_ref, *refs):
    *refs, out_ref, place_ref, split_ref, sem = refs
    copy = pltpu.make_async_copy(matrix_ref.at[pl.ds(0, out_ref.shape[0])], out_ref, sem)
    copy.start()
    pick_count, row_count = refs[1].shape
    spread = spread_of(pick_count, row_count)
    items = pick_count * row_count

    def marked(at):
        marks = lax.dot_general(
            jnp.where(at, 1.0, 0.0).astype(jnp.bfloat16),
            spread,
            (((1,), (1,)), ((), ())),
            preferred_element_type=jnp.float32,
        )
        return jnp.where(marks > 0.0, 1.0, 0.0)

    for s in range(lane_count):
        lists_ref, picks_ref = refs[2 * s : 2 * s + 2]
        number, slot, _ = route(node_count, lane_count, lists_ref[...], picks_ref[...], spread)
        target = target_of(node_count, lane_count, capacity, s, number, slot)
        place_ref[:, s * row_count : (s + 1) * row_count] = marked(
            iota((place_ref.shape[0], items), 0) == target
        )
        if s == 0:
            for q in range(lane_count):
                lane = lax.rem(lax.axis_index("lane") + q, lane_count)
                there = number == number_of(node_count, lane_count, lane, split)
                split_ref[q * capacity : (q + 1) * capacity, :] = marked(
                    iota((capacity, items), 0) == jnp.where(there, slot, -1)
                )
    copy.wait()


def own_kernel(*refs):
    *received_refs, first_ref, matrix_ref, out_ref, second_ref, sem = refs
    depth, width = matrix_ref.shape
    head = first_ref.shape[0]
    copy = pltpu.make_async_copy(matrix_ref.at[pl.ds(head, depth - head)], second_ref, sem)
    copy.start()
    rows = jnp.concatenate([received_ref[:, :depth] for received_ref in received_refs], axis=0)
    for start in range(0, width, TILE):
        columns = slice(start, start + TILE)
        out_ref[:, columns] = jnp.dot(
            rows[:, :head], first_ref[:, columns], preferred_element_type=jnp.float32
        )
    copy.wait()
    for start in range(0, width, TILE):
        columns = slice(start, start + TILE)
        out_ref[:, columns] += jnp.dot(
            rows[:, head:], second_ref[:, columns], preferred_element_type=jnp.float32
        )


def other_kernel(turns, *refs):
    received_refs = refs[:turns]
    own_ref, weight_ref, *out_refs = refs[turns:]
    depth, width = weight_ref.shape
    rows = jnp.concatenate([received_ref[:, depth:] for received_ref in received_refs], axis=0)

    for start in range(0, width, TILE):
        columns = slice(start, start + TILE)
        part = jnp.dot(rows, weight_ref[:, columns], preferred_element_type=jnp.float32)
        total = own_ref[:, columns] + part
        start_row = 0
        for out_ref in out_refs:
            rows_here = out_ref.shape[0]
            out_ref[:, columns] = total[start_row : start_row + rows_here].astype(jnp.bfloat16)
            start_row += rows_here


def sum_kernel(split, pieces, place_ref, *refs):
    *refs, all_ref = refs
    returned_refs, own_ref, other_refs = refs[:-1-pieces], refs[-1-pieces], refs[-pieces:]
    block = returned_refs[0].shape[0]
    rows = own_ref.shape[0]
    for i, returned_ref in enumerate(returned_refs):
        all_ref[i * block : (i + 1) * block, :] = returned_ref[...]
    place = place_ref[...]
    place = jnp.concatenate([place[: split * block], place[(split + 1) * block :]], axis=0)
    total = lax.dot_general(
        place.astype(jnp.bfloat16),
        all_ref[...],
        (((0,), (0,)), ((), ())),
        preferred_element_type=jnp.float32,
    )
    own_ref[...] = total[:rows]
    start = 0
    for other_ref in other_refs:
        other_ref[...] = total[rows:, start : start + other_ref.shape[1]].astype(other_ref.dtype)
        start += other_ref.shape[1]


def last_kernel(pieces, own_ref, place_ref, *refs):
    other_refs, returned_refs, out_ref = refs[:pieces], refs[pieces:-1], refs[-1]
    slots = returned_refs[0].shape[0]
    total = own_ref[...] + jnp.concatenate([other_ref[...].astype(jnp.float32) for other_ref in other_refs], axis=1)
    for i, returned_ref in enumerate(returned_refs):
        total = total + lax.dot_general(
            place_ref[i * slots : (i + 1) * slots, :].astype(jnp.bfloat16),
            returned_ref[...],
            (((0,), (0,)), ((), ())),
            preferred_element_type=jnp.float32,
        )
    out_ref[...] = total.astype(jnp.bfloat16)


def local(
    expert_hidden,
    gate_scores,
    node_lists,
    expert_picks,
    routed_down,
    query_latent,
    query_rope,
    cache_latent,
    cache_rope,
    cache_lengths,
):
    node_count = lax.axis_size("node")
    lane_count = lax.axis_size("lane")
    row_count, _, hidden_width = expert_hidden.shape
    width = routed_down.shape[2]
    capacity = max(
        2, min(row_count // 2, 2 * ((row_count * NODES_TOP + node_count - 1) // node_count))
    )
    turns = node_count // lane_count
    block = lane_count * capacity
    slots = turns * block

    def other_core(value):
        return lax.ppermute(value, "lane", [(0, 1), (1, 0)])

    def meet(value, turn, across=0):
        pairs = []
        for node in range(node_count):
            for lane in range(lane_count):
                there = partner(node_count, node, number_of(node_count, lane_count, lane, turn))
                pairs.append((node * lane_count + lane, there * lane_count + (lane + across) % lane_count))
        return lax.ppermute(value, ("node", "lane"), pairs)

    whole = pl.BlockSpec(memory_space=pltpu.VMEM)
    outside = pl.BlockSpec(memory_space=pltpu.HBM)

    def in_hbm(value):
        return pltpu.with_memory_space_constraint(value, pltpu.HBM)

    def in_vmem(value):
        return pltpu.with_memory_space_constraint(value, pltpu.VMEM)

    def params(mib):
        return pltpu.CompilerParams(vmem_limit_bytes=mib * MIB)

    own_matrix = routed_down[0]
    mine = [gate_scores.T, node_lists.T, expert_picks.T, expert_hidden.reshape(-1, hidden_width)]
    theirs = [other_core(value) for value in mine]
    mine = pl.pallas_call(
        load_kernel,
        in_specs=[outside] * 4,
        out_specs=[whole] * 4,
        out_shape=[pltpu.VMEM(value.shape, value.dtype) for value in mine],
        scratch_shapes=[pltpu.SemaphoreType.DMA((4,))],
        compiler_params=params(1),
        name="load",
    )(*[in_hbm(value) for value in mine])
    sent_matrix, *_ = lax.optimization_barrier((own_matrix, *theirs, mine[0]))
    other_matrix = other_core(sent_matrix)
    split = turns // 2 - 1
    send = pl.pallas_call(
        functools.partial(pack_kernel, node_count, lane_count, capacity),
        in_specs=[whole] * 8,
        out_specs=[whole] * turns,
        out_shape=[jax.ShapeDtypeStruct((block, lane_count * hidden_width), jnp.bfloat16)] * turns,
        compiler_params=params(4),
        name="pack",
    )(*[in_vmem(value) for value in (*mine, *theirs)])
    received = [meet(value, turn) for turn, value in enumerate(send)]
    late_matrix, _ = lax.optimization_barrier((own_matrix, send[-1]))
    head = hidden_width * 3 // 4
    first, place, split_place = pl.pallas_call(
        functools.partial(fetch_kernel, node_count, lane_count, capacity, split),
        in_specs=[outside] + [whole] * 4,
        out_specs=[whole] * 3,
        out_shape=[
            pltpu.VMEM((head, width), own_matrix.dtype),
            jax.ShapeDtypeStruct((slots, lane_count * row_count), jnp.float32),
            jax.ShapeDtypeStruct((block, row_count), jnp.float32),
        ],
        scratch_shapes=[pltpu.SemaphoreType.DMA],
        compiler_params=params(2),
        cost_estimate=pl.CostEstimate(flops=0, bytes_accessed=4 * head * width, transcendentals=0),
        name="fetch",
    )(in_hbm(late_matrix), *[in_vmem(value) for value in (*mine[1:3], *theirs[1:3])])
    own_part = pl.pallas_call(
        own_kernel,
        in_specs=[whole] * (turns + 1) + [outside],
        out_specs=whole,
        out_shape=jax.ShapeDtypeStruct((slots, width), jnp.float32),
        scratch_shapes=[
            pltpu.VMEM((hidden_width - head, width), own_matrix.dtype),
            pltpu.SemaphoreType.DMA,
        ],
        compiler_params=params(8),
        name="own",
    )(*received, in_vmem(first), in_hbm(late_matrix))
    pieces = [block] * split + [capacity] * lane_count + [block] * (turns - split - 1)
    output = pl.pallas_call(
        functools.partial(other_kernel, turns),
        in_specs=[whole] * (turns + 2),
        out_specs=[whole] * len(pieces),
        out_shape=[jax.ShapeDtypeStruct((rows, width), jnp.bfloat16) for rows in pieces],
        compiler_params=params(2),
        name="other",
    )(*received, in_vmem(own_part), in_vmem(other_matrix))
    returned = [meet(value, turn) for turn, value in enumerate(output[:split])]
    last = [meet(output[split + across], split, across) for across in range(lane_count)]
    returned += [meet(value, turn) for turn, value in enumerate(output[split + lane_count :], split + 1)]
    query_latent, query_rope, cache_latent, cache_rope, cache_lengths, _ = lax.optimization_barrier(
        (query_latent, query_rope, cache_latent, cache_rope, cache_lengths, output[-1])
    )
    context = attend(query_latent, query_rope, cache_latent, cache_rope, cache_lengths)
    *returned, context = lax.optimization_barrier((*returned, context))
    tiles = width // 128
    widths = [128 * ((i + 1) * tiles // 3 - i * tiles // 3) for i in range(3)]
    own, *others = pl.pallas_call(
        functools.partial(sum_kernel, split, len(widths)),
        in_specs=[whole] * turns,
        out_specs=[whole] * (1 + len(widths)),
        out_shape=[jax.ShapeDtypeStruct((row_count, width), jnp.float32)]
        + [jax.ShapeDtypeStruct((row_count, piece), jnp.bfloat16) for piece in widths],
        scratch_shapes=[pltpu.VMEM((slots - block, width), jnp.bfloat16)],
        compiler_params=params(8),
        cost_estimate=pl.CostEstimate(flops=0, bytes_accessed=0, transcendentals=0),
        name="sum",
    )(place, *returned)
    others = [in_vmem(other_core(value)) for value in others]
    moe_out = pl.pallas_call(
        functools.partial(last_kernel, len(widths)),
        in_specs=[whole] * (2 + len(widths) + lane_count),
        out_specs=whole,
        out_shape=jax.ShapeDtypeStruct((row_count, width), jnp.bfloat16),
        compiler_params=params(2),
        name="last",
    )(in_vmem(own), split_place, *others, *[in_vmem(value) for value in last])
    return (moe_out, context)


def solution(mesh):
    placed = (
        P(("groups", "node", "lane"), None, None),
        P(("groups", "node", "lane"), None),
        P(("groups", "node", "lane"), None),
        P(("groups", "node", "lane"), None),
        P(("node", "lane"), None, None),
        P(("groups", "node", "lane"), None, None),
        P(("groups", "node", "lane"), None),
        P(("groups", "node", "lane"), None, None),
        P(("groups", "node", "lane"), None, None),
        P(("groups", "node", "lane")),
    )
    return jax.shard_map(
        local,
        mesh=mesh,
        in_specs=placed,
        out_specs=(P(("groups", "node", "lane"), None), P(("groups", "node", "lane"), None, None)),
        check_vma=False,
    )
```

```python
import functools

import jax
import jax.numpy as jnp
from jax import lax
from jax.experimental import pallas as pl
from jax.experimental.pallas import tpu as pltpu
from jax.sharding import PartitionSpec as P

NODES_TOP = 4
MIB = 2**20
TILE = 512


score_scale = 192.0 ** (-0.5)
route_scale = 2.5


def attend_kernel(lengths_ref, latent_ref, rope_ref, keys_ref, rope_keys_ref, out_ref):
    row_count, head_count, _ = latent_ref.shape
    rope_width, position_count = rope_keys_ref.shape[1:]
    lanes = max(128, rope_width)
    heads = lanes // rope_width
    groups = rope_ref.shape[1] // lanes
    rope = rope_ref[...].astype(jnp.float32)
    rope = jnp.concatenate([rope[:, i * lanes : (i + 1) * lanes] for i in range(groups)], axis=0)
    shape = (row_count * head_count, groups * row_count)
    head = lax.rem(iota(shape, 0), head_count)
    picked = iota(shape, 1) == head // heads * row_count + iota(shape, 0) // head_count
    rope = exact(jnp.where(picked, 1.0, 0.0), rope)
    kept = iota(rope.shape, 1) // rope_width == lax.rem(iota(rope.shape, 0), heads)
    rope = jnp.where(kept, rope, 0.0).astype(jnp.bfloat16)
    scores = []
    for row in range(row_count):
        score = lax.dot_general(
            latent_ref[row], keys_ref[row], (((1,), (1,)), ((), ())), preferred_element_type=jnp.float32
        )
        rope_keys = jnp.concatenate([rope_keys_ref[row]] * heads, axis=0)
        score = score + jnp.dot(
            rope[row * head_count : (row + 1) * head_count], rope_keys, preferred_element_type=jnp.float32
        )
        valid = iota(score.shape, 1) < lengths_ref[row]
        scores.append(jnp.where(valid, score * score_scale, -jnp.inf))
    scores = jnp.concatenate(scores, axis=0)
    expd = jnp.exp(scores - jnp.max(scores, axis=-1, keepdims=True))
    probs = (expd / jnp.sum(expd, axis=-1, keepdims=True)).astype(jnp.bfloat16)
    for row in range(row_count):
        context = jnp.dot(
            probs[row * head_count : (row + 1) * head_count], keys_ref[row], preferred_element_type=jnp.float32
        )
        out_ref[row] = context.astype(jnp.bfloat16)


def attend(query_latent, query_rope, cache_latent, cache_rope, cache_lengths):
    return pl.pallas_call(
        attend_kernel,
        in_specs=[pl.BlockSpec(memory_space=pltpu.SMEM)] + [pl.BlockSpec(memory_space=pltpu.VMEM)] * 4,
        out_specs=pl.BlockSpec(memory_space=pltpu.VMEM),
        out_shape=jax.ShapeDtypeStruct(query_latent.shape, jnp.bfloat16),
        compiler_params=pltpu.CompilerParams(vmem_limit_bytes=8 * MIB),
        name="attend",
    )(cache_lengths, query_latent, query_rope, cache_latent, cache_rope)


def iota(shape, dim):
    return lax.broadcasted_iota(jnp.int32, shape, dim)


def exact(a, b):
    return jnp.dot(a.astype(jnp.bfloat16), b.astype(jnp.bfloat16), preferred_element_type=jnp.float32)


def meeting(node_count, a, b):
    return a ^ b if node_count & (node_count - 1) == 0 else (a + b) % node_count


def partner(node_count, a, number):
    return a ^ number if node_count & (node_count - 1) == 0 else (number - a) % node_count


def turn_of(node_count, lane_count, lane, number):
    far = node_count // lane_count // 2
    turn = (node_count - 1 - number) // lane_count
    turn = jnp.where((lane == 0) & (turn < far), far - 1 - turn, turn)
    return jnp.where(number % lane_count == lane, turn, -1)


def number_of(node_count, lane_count, lane, turn):
    far = node_count // lane_count // 2
    if turn < far:
        turn = jnp.where(lane == 0, far - 1 - turn, turn) if isinstance(lane, jax.Array) else (turn, far - 1 - turn)[lane == 0]
    return node_count - lane_count * (turn + 1) + lane


def load_kernel(*refs):
    *refs, sems = refs
    half = len(refs) // 2
    copies = [
        pltpu.make_async_copy(in_ref, out_ref, sems.at[i])
        for i, (in_ref, out_ref) in enumerate(zip(refs[:half], refs[half:]))
    ]
    for copy in copies:
        copy.start()
    for copy in copies:
        copy.wait()


def spread_of(pick_count, row_count):
    items = pick_count * row_count
    spread = iota((row_count, items), 1) // pick_count == iota((row_count, items), 0)
    return jnp.where(spread, 1.0, 0.0).astype(jnp.bfloat16)


def flat(values, spread):
    pick_count, _ = values.shape
    _, items = spread.shape
    own_pick = lax.rem(iota((pick_count, items), 1), pick_count) == iota((pick_count, items), 0)
    return jnp.sum(jnp.where(own_pick, exact(values, spread), 0.0), axis=0, keepdims=True)


def route(node_count, lane_count, lists, picks, spread):
    _, row_count = picks.shape
    _, items = spread.shape
    lane_here = lax.axis_index("lane")
    before = iota((row_count, row_count), 0) < iota((row_count, row_count), 1)
    nodes = iota((node_count, row_count), 0)
    choice = picks // lane_count
    order = lax.rem(picks - choice * lane_count - lane_here + lane_count, lane_count)
    node = jnp.zeros_like(picks)
    member = jnp.zeros((node_count, row_count), jnp.float32)
    for j in range(lists.shape[0]):
        node = jnp.where(choice == j, lists[j : j + 1, :], node)
        member = jnp.where(nodes == lists[j : j + 1, :], 1.0, member)
    earlier = exact(exact(member, jnp.where(before, 1.0, 0.0)), spread)
    both = flat((node * lane_count + order).astype(jnp.float32), spread).astype(jnp.int32)
    node = both // lane_count
    order = both - node * lane_count
    named = iota((node_count, items), 0) == node
    slot = jnp.sum(jnp.where(named, earlier, 0.0), axis=0, keepdims=True).astype(jnp.int32)
    return meeting(node_count, lax.axis_index("node"), node), slot, order


def target_of(node_count, lane_count, capacity, source, number, slot):
    turn = turn_of(node_count, lane_count, lax.axis_index("lane"), number)
    return jnp.where(turn >= 0, (turn * lane_count + source) * capacity + slot, -1)


def pack_kernel(node_count, lane_count, capacity, *refs):
    sources = [refs[4 * s : 4 * s + 4] for s in range(lane_count)]
    send_refs = refs[4 * lane_count :]
    block = lane_count * capacity
    slots = len(send_refs) * block
    hidden_width = sources[0][3].shape[1]
    spread = spread_of(*sources[0][0].shape)
    places = iota((slots, spread.shape[1]), 0)
    parts = [None] * lane_count
    for s, (scores_ref, lists_ref, picks_ref, hidden_ref) in enumerate(sources):
        scores = scores_ref[...]
        combine = (route_scale * scores / jnp.sum(scores, axis=0, keepdims=True)).astype(jnp.bfloat16)
        weight = flat(combine, spread)
        number, slot, order = route(node_count, lane_count, lists_ref[...], picks_ref[...], spread)
        at = places == target_of(node_count, lane_count, capacity, s, number, slot)
        hidden = hidden_ref[...]
        for q in range(lane_count):
            placing = jnp.where(at & (order == q), weight, 0.0).astype(jnp.bfloat16)
            part = jnp.dot(placing, hidden, preferred_element_type=jnp.float32)
            parts[q] = part if parts[q] is None else parts[q] + part
    for q in range(lane_count):
        columns = slice(q * hidden_width, (q + 1) * hidden_width)
        for turn, send_ref in enumerate(send_refs):
            send_ref[:, columns] = parts[q][turn * block : (turn + 1) * block].astype(jnp.bfloat16)


def place_kernel(node_count, lane_count, capacity, split, *refs):
    *refs, place_ref, split_ref = refs
    pick_count, row_count = refs[1].shape
    spread = spread_of(pick_count, row_count)
    items = pick_count * row_count

    def marked(at):
        marks = lax.dot_general(
            jnp.where(at, 1.0, 0.0).astype(jnp.bfloat16),
            spread,
            (((1,), (1,)), ((), ())),
            preferred_element_type=jnp.float32,
        )
        return jnp.where(marks > 0.0, 1.0, 0.0)

    for s in range(lane_count):
        lists_ref, picks_ref = refs[2 * s : 2 * s + 2]
        number, slot, _ = route(node_count, lane_count, lists_ref[...], picks_ref[...], spread)
        target = target_of(node_count, lane_count, capacity, s, number, slot)
        place_ref[:, s * row_count : (s + 1) * row_count] = marked(
            iota((place_ref.shape[0], items), 0) == target
        )
        if s == 0:
            for q in range(lane_count):
                lane = lax.rem(lax.axis_index("lane") + q, lane_count)
                there = number == number_of(node_count, lane_count, lane, split)
                split_ref[q * capacity : (q + 1) * capacity, :] = marked(
                    iota((capacity, items), 0) == jnp.where(there, slot, -1)
                )


def own_kernel(*refs):
    *received_refs, matrix_ref, out_ref = refs
    depth, width = matrix_ref.shape
    rows = jnp.concatenate([received_ref[:, :depth] for received_ref in received_refs], axis=0)
    for start in range(0, width, TILE):
        columns = slice(start, start + TILE)
        out_ref[:, columns] = jnp.dot(rows, matrix_ref[:, columns], preferred_element_type=jnp.float32)


def other_kernel(turns, *refs):
    received_refs = refs[:turns]
    own_ref, weight_ref, *out_refs = refs[turns:]
    depth, width = weight_ref.shape
    rows = jnp.concatenate([received_ref[:, depth:] for received_ref in received_refs], axis=0)

    for start in range(0, width, TILE):
        columns = slice(start, start + TILE)
        part = jnp.dot(rows, weight_ref[:, columns], preferred_element_type=jnp.float32)
        total = own_ref[:, columns] + part
        start_row = 0
        for out_ref in out_refs:
            rows_here = out_ref.shape[0]
            out_ref[:, columns] = total[start_row : start_row + rows_here].astype(jnp.bfloat16)
            start_row += rows_here


def sum_kernel(split, pieces, place_ref, *refs):
    *refs, all_ref = refs
    returned_refs, own_ref, other_refs = refs[:-1-pieces], refs[-1-pieces], refs[-pieces:]
    block = returned_refs[0].shape[0]
    rows = own_ref.shape[0]
    for i, returned_ref in enumerate(returned_refs):
        all_ref[i * block : (i + 1) * block, :] = returned_ref[...]
    place = place_ref[...]
    place = jnp.concatenate([place[: split * block], place[(split + 1) * block :]], axis=0)
    total = lax.dot_general(
        place.astype(jnp.bfloat16),
        all_ref[...],
        (((0,), (0,)), ((), ())),
        preferred_element_type=jnp.float32,
    )
    own_ref[...] = total[:rows]
    start = 0
    for other_ref in other_refs:
        other_ref[...] = total[rows:, start : start + other_ref.shape[1]].astype(other_ref.dtype)
        start += other_ref.shape[1]


def last_kernel(pieces, own_ref, place_ref, *refs):
    other_refs, returned_refs, out_ref = refs[:pieces], refs[pieces:-1], refs[-1]
    slots = returned_refs[0].shape[0]
    total = own_ref[...] + jnp.concatenate([other_ref[...].astype(jnp.float32) for other_ref in other_refs], axis=1)
    for i, returned_ref in enumerate(returned_refs):
        total = total + lax.dot_general(
            place_ref[i * slots : (i + 1) * slots, :].astype(jnp.bfloat16),
            returned_ref[...],
            (((0,), (0,)), ((), ())),
            preferred_element_type=jnp.float32,
        )
    out_ref[...] = total.astype(jnp.bfloat16)


def local(
    expert_hidden,
    gate_scores,
    node_lists,
    expert_picks,
    routed_down,
    query_latent,
    query_rope,
    cache_latent,
    cache_rope,
    cache_lengths,
):
    node_count = lax.axis_size("node")
    lane_count = lax.axis_size("lane")
    row_count, _, hidden_width = expert_hidden.shape
    width = routed_down.shape[2]
    capacity = max(
        2, min(row_count // 2, 2 * ((row_count * NODES_TOP + node_count - 1) // node_count))
    )
    turns = node_count // lane_count
    block = lane_count * capacity
    slots = turns * block

    def other_core(value):
        return lax.ppermute(value, "lane", [(0, 1), (1, 0)])

    def meet(value, turn, across=0):
        pairs = []
        for node in range(node_count):
            for lane in range(lane_count):
                there = partner(node_count, node, number_of(node_count, lane_count, lane, turn))
                pairs.append((node * lane_count + lane, there * lane_count + (lane + across) % lane_count))
        return lax.ppermute(value, ("node", "lane"), pairs)

    whole = pl.BlockSpec(memory_space=pltpu.VMEM)
    outside = pl.BlockSpec(memory_space=pltpu.HBM)

    def in_hbm(value):
        return pltpu.with_memory_space_constraint(value, pltpu.HBM)

    def in_vmem(value):
        return pltpu.with_memory_space_constraint(value, pltpu.VMEM)

    def params(mib):
        return pltpu.CompilerParams(vmem_limit_bytes=mib * MIB)

    own_matrix = routed_down[0]
    mine = [gate_scores.T, node_lists.T, expert_picks.T, expert_hidden.reshape(-1, hidden_width)]
    theirs = [other_core(value) for value in mine]
    mine = pl.pallas_call(
        load_kernel,
        in_specs=[outside] * 4,
        out_specs=[whole] * 4,
        out_shape=[pltpu.VMEM(value.shape, value.dtype) for value in mine],
        scratch_shapes=[pltpu.SemaphoreType.DMA((4,))],
        compiler_params=params(1),
        name="load",
    )(*[in_hbm(value) for value in mine])
    sent_matrix, *_ = lax.optimization_barrier((own_matrix, *theirs, mine[0]))
    other_matrix = other_core(sent_matrix)
    split = turns // 2 - 1
    send = pl.pallas_call(
        functools.partial(pack_kernel, node_count, lane_count, capacity),
        in_specs=[whole] * 8,
        out_specs=[whole] * turns,
        out_shape=[jax.ShapeDtypeStruct((block, lane_count * hidden_width), jnp.bfloat16)] * turns,
        compiler_params=params(4),
        cost_estimate=pl.CostEstimate(flops=6 * 10**9, bytes_accessed=0, transcendentals=0),
        name="pack",
    )(*[in_vmem(value) for value in (*mine, *theirs)])
    received = [meet(value, turn) for turn, value in enumerate(send)]
    *attention, _ = lax.optimization_barrier(
        (query_latent, query_rope, cache_latent, cache_rope, cache_lengths, send[-1])
    )
    context = attend(*attention)
    *received, context = lax.optimization_barrier((*received, context))
    own_part = pl.pallas_call(
        own_kernel,
        in_specs=[whole] * (turns + 1),
        out_specs=whole,
        out_shape=jax.ShapeDtypeStruct((slots, width), jnp.float32),
        compiler_params=params(2),
        name="own",
    )(*received, in_vmem(own_matrix))
    pieces = [block] * split + [capacity] * lane_count + [block] * (turns - split - 1)
    output = pl.pallas_call(
        functools.partial(other_kernel, turns),
        in_specs=[whole] * (turns + 2),
        out_specs=[whole] * len(pieces),
        out_shape=[jax.ShapeDtypeStruct((rows, width), jnp.bfloat16) for rows in pieces],
        compiler_params=params(2),
        name="other",
    )(*received, in_vmem(own_part), in_vmem(other_matrix))
    returned = [meet(value, turn) for turn, value in enumerate(output[:split])]
    last = [meet(output[split + across], split, across) for across in range(lane_count)]
    returned += [meet(value, turn) for turn, value in enumerate(output[split + lane_count :], split + 1)]
    late, _ = lax.optimization_barrier((mine[1], output[-1]))
    place, split_place = pl.pallas_call(
        functools.partial(place_kernel, node_count, lane_count, capacity, split),
        in_specs=[whole] * 4,
        out_specs=[whole] * 2,
        out_shape=[
            jax.ShapeDtypeStruct((slots, lane_count * row_count), jnp.float32),
            jax.ShapeDtypeStruct((block, row_count), jnp.float32),
        ],
        compiler_params=params(2),
        name="place",
    )(*[in_vmem(value) for value in (late, mine[2], *theirs[1:3])])
    tiles = width // 128
    widths = [128 * ((i + 1) * tiles // 3 - i * tiles // 3) for i in range(3)]
    own, *others = pl.pallas_call(
        functools.partial(sum_kernel, split, len(widths)),
        in_specs=[whole] * turns,
        out_specs=[whole] * (1 + len(widths)),
        out_shape=[jax.ShapeDtypeStruct((row_count, width), jnp.float32)]
        + [jax.ShapeDtypeStruct((row_count, piece), jnp.bfloat16) for piece in widths],
        scratch_shapes=[pltpu.VMEM((slots - block, width), jnp.bfloat16)],
        compiler_params=params(8),
        cost_estimate=pl.CostEstimate(flops=0, bytes_accessed=0, transcendentals=0),
        name="sum",
    )(place, *returned)
    others = [in_vmem(other_core(value)) for value in others]
    moe_out = pl.pallas_call(
        functools.partial(last_kernel, len(widths)),
        in_specs=[whole] * (2 + len(widths) + lane_count),
        out_specs=whole,
        out_shape=jax.ShapeDtypeStruct((row_count, width), jnp.bfloat16),
        compiler_params=params(2),
        name="last",
    )(in_vmem(own), split_place, *others, *[in_vmem(value) for value in last])
    return (moe_out, context)


def solution(mesh):
    placed = (
        P(("groups", "node", "lane"), None, None),
        P(("groups", "node", "lane"), None),
        P(("groups", "node", "lane"), None),
        P(("groups", "node", "lane"), None),
        P(("node", "lane"), None, None),
        P(("groups", "node", "lane"), None, None),
        P(("groups", "node", "lane"), None),
        P(("groups", "node", "lane"), None, None),
        P(("groups", "node", "lane"), None, None),
        P(("groups", "node", "lane")),
    )
    return jax.shard_map(
        local,
        mesh=mesh,
        in_specs=placed,
        out_specs=(P(("groups", "node", "lane"), None), P(("groups", "node", "lane"), None, None)),
        check_vma=False,
    )
```

```python
import functools

import jax
import jax.numpy as jnp
from jax import lax
from jax.experimental import pallas as pl
from jax.experimental.pallas import tpu as pltpu
from jax.sharding import PartitionSpec as P

NODES_TOP = 4
MIB = 2**20
TILE = 512


score_scale = 192.0 ** (-0.5)
route_scale = 2.5


def attend_kernel(lengths_ref, latent_ref, rope_ref, keys_ref, rope_keys_ref, out_ref):
    row_count, head_count, _ = latent_ref.shape
    rope_width, position_count = rope_keys_ref.shape[1:]
    lanes = max(128, rope_width)
    heads = lanes // rope_width
    groups = rope_ref.shape[1] // lanes
    rope = rope_ref[...].astype(jnp.float32)
    rope = jnp.concatenate([rope[:, i * lanes : (i + 1) * lanes] for i in range(groups)], axis=0)
    shape = (row_count * head_count, groups * row_count)
    head = lax.rem(iota(shape, 0), head_count)
    picked = iota(shape, 1) == head // heads * row_count + iota(shape, 0) // head_count
    rope = exact(jnp.where(picked, 1.0, 0.0), rope)
    kept = iota(rope.shape, 1) // rope_width == lax.rem(iota(rope.shape, 0), heads)
    rope = jnp.where(kept, rope, 0.0).astype(jnp.bfloat16)
    scores = []
    for row in range(row_count):
        score = lax.dot_general(
            latent_ref[row], keys_ref[row], (((1,), (1,)), ((), ())), preferred_element_type=jnp.float32
        )
        rope_keys = jnp.concatenate([rope_keys_ref[row]] * heads, axis=0)
        score = score + jnp.dot(
            rope[row * head_count : (row + 1) * head_count], rope_keys, preferred_element_type=jnp.float32
        )
        valid = iota(score.shape, 1) < lengths_ref[row]
        scores.append(jnp.where(valid, score * score_scale, -jnp.inf))
    scores = jnp.concatenate(scores, axis=0)
    expd = jnp.exp(scores - jnp.max(scores, axis=-1, keepdims=True))
    probs = (expd / jnp.sum(expd, axis=-1, keepdims=True)).astype(jnp.bfloat16)
    for row in range(row_count):
        context = jnp.dot(
            probs[row * head_count : (row + 1) * head_count], keys_ref[row], preferred_element_type=jnp.float32
        )
        out_ref[row] = context.astype(jnp.bfloat16)


def attend(query_latent, query_rope, cache_latent, cache_rope, cache_lengths):
    return pl.pallas_call(
        attend_kernel,
        in_specs=[pl.BlockSpec(memory_space=pltpu.SMEM)] + [pl.BlockSpec(memory_space=pltpu.VMEM)] * 4,
        out_specs=pl.BlockSpec(memory_space=pltpu.VMEM),
        out_shape=jax.ShapeDtypeStruct(query_latent.shape, jnp.bfloat16),
        compiler_params=pltpu.CompilerParams(vmem_limit_bytes=8 * MIB),
        name="attend",
    )(cache_lengths, query_latent, query_rope, cache_latent, cache_rope)


def iota(shape, dim):
    return lax.broadcasted_iota(jnp.int32, shape, dim)


def exact(a, b):
    return jnp.dot(a.astype(jnp.bfloat16), b.astype(jnp.bfloat16), preferred_element_type=jnp.float32)


def meeting(node_count, a, b):
    return a ^ b if node_count & (node_count - 1) == 0 else (a + b) % node_count


def partner(node_count, a, number):
    return a ^ number if node_count & (node_count - 1) == 0 else (number - a) % node_count


def turn_of(node_count, lane_count, lane, number):
    half = node_count // 2
    far_turn = (number - half) // lane_count
    far_lane = (number - half + lane_count - 1 + far_turn * (lane_count - 1)) % lane_count
    near_turn = (node_count - 1 - number) // lane_count
    turn = jnp.where(number >= half, far_turn, near_turn)
    return jnp.where(jnp.where(number >= half, far_lane, number % lane_count) == lane, turn, -1)


def number_of(node_count, lane_count, lane, turn):
    half = node_count // 2
    if turn < half // lane_count:
        return half + lane_count * turn + (turn + 1 + lane) % lane_count
    return node_count - lane_count * (turn + 1) + lane


def load_kernel(*refs):
    *refs, sems = refs
    half = len(refs) // 2
    copies = [
        pltpu.make_async_copy(in_ref, out_ref, sems.at[i])
        for i, (in_ref, out_ref) in enumerate(zip(refs[:half], refs[half:]))
    ]
    for copy in copies:
        copy.start()
    for copy in copies:
        copy.wait()


def spread_of(pick_count, row_count):
    items = pick_count * row_count
    spread = iota((row_count, items), 1) // pick_count == iota((row_count, items), 0)
    return jnp.where(spread, 1.0, 0.0).astype(jnp.bfloat16)


def flat(values, spread):
    pick_count, _ = values.shape
    _, items = spread.shape
    own_pick = lax.rem(iota((pick_count, items), 1), pick_count) == iota((pick_count, items), 0)
    return jnp.sum(jnp.where(own_pick, exact(values, spread), 0.0), axis=0, keepdims=True)


def route(node_count, lane_count, lists, picks, spread):
    _, row_count = picks.shape
    _, items = spread.shape
    lane_here = lax.axis_index("lane")
    before = iota((row_count, row_count), 0) < iota((row_count, row_count), 1)
    nodes = iota((node_count, row_count), 0)
    choice = picks // lane_count
    order = lax.rem(picks - choice * lane_count - lane_here + lane_count, lane_count)
    node = jnp.zeros_like(picks)
    member = jnp.zeros((node_count, row_count), jnp.float32)
    for j in range(lists.shape[0]):
        node = jnp.where(choice == j, lists[j : j + 1, :], node)
        member = jnp.where(nodes == lists[j : j + 1, :], 1.0, member)
    earlier = exact(exact(member, jnp.where(before, 1.0, 0.0)), spread)
    both = flat((node * lane_count + order).astype(jnp.float32), spread).astype(jnp.int32)
    node = both // lane_count
    order = both - node * lane_count
    named = iota((node_count, items), 0) == node
    slot = jnp.sum(jnp.where(named, earlier, 0.0), axis=0, keepdims=True).astype(jnp.int32)
    return meeting(node_count, lax.axis_index("node"), node), slot, order


def target_of(node_count, lane_count, capacity, source, number, slot):
    turn = turn_of(node_count, lane_count, lax.axis_index("lane"), number)
    return jnp.where(turn >= 0, (turn * lane_count + source) * capacity + slot, -1)


def pack_kernel(node_count, lane_count, capacity, *refs):
    sources = [refs[4 * s : 4 * s + 4] for s in range(lane_count)]
    send_refs = refs[4 * lane_count :]
    block = lane_count * capacity
    slots = len(send_refs) * block
    hidden_width = sources[0][3].shape[1]
    spread = spread_of(*sources[0][0].shape)
    places = iota((slots, spread.shape[1]), 0)
    parts = [None] * lane_count
    for s, (scores_ref, lists_ref, picks_ref, hidden_ref) in enumerate(sources):
        scores = scores_ref[...]
        combine = (route_scale * scores / jnp.sum(scores, axis=0, keepdims=True)).astype(jnp.bfloat16)
        weight = flat(combine, spread)
        number, slot, order = route(node_count, lane_count, lists_ref[...], picks_ref[...], spread)
        at = places == target_of(node_count, lane_count, capacity, s, number, slot)
        hidden = hidden_ref[...]
        for q in range(lane_count):
            placing = jnp.where(at & (order == q), weight, 0.0).astype(jnp.bfloat16)
            part = jnp.dot(placing, hidden, preferred_element_type=jnp.float32)
            parts[q] = part if parts[q] is None else parts[q] + part
    for q in range(lane_count):
        columns = slice(q * hidden_width, (q + 1) * hidden_width)
        for turn, send_ref in enumerate(send_refs):
            send_ref[:, columns] = parts[q][turn * block : (turn + 1) * block].astype(jnp.bfloat16)


def place_kernel(node_count, lane_count, capacity, split, *refs):
    *refs, place_ref, split_ref = refs
    pick_count, row_count = refs[1].shape
    spread = spread_of(pick_count, row_count)
    items = pick_count * row_count

    def marked(at):
        marks = lax.dot_general(
            jnp.where(at, 1.0, 0.0).astype(jnp.bfloat16),
            spread,
            (((1,), (1,)), ((), ())),
            preferred_element_type=jnp.float32,
        )
        return jnp.where(marks > 0.0, 1.0, 0.0)

    for s in range(lane_count):
        lists_ref, picks_ref = refs[2 * s : 2 * s + 2]
        number, slot, _ = route(node_count, lane_count, lists_ref[...], picks_ref[...], spread)
        target = target_of(node_count, lane_count, capacity, s, number, slot)
        place_ref[:, s * row_count : (s + 1) * row_count] = marked(
            iota((place_ref.shape[0], items), 0) == target
        )
        if s == 0:
            for q in range(lane_count):
                lane = lax.rem(lax.axis_index("lane") + q, lane_count)
                there = number == number_of(node_count, lane_count, lane, split)
                split_ref[q * capacity : (q + 1) * capacity, :] = marked(
                    iota((capacity, items), 0) == jnp.where(there, slot, -1)
                )


def own_kernel(*refs):
    *received_refs, matrix_ref, out_ref = refs
    depth, width = matrix_ref.shape
    rows = jnp.concatenate([received_ref[:, :depth] for received_ref in received_refs], axis=0)
    for start in range(0, width, TILE):
        columns = slice(start, start + TILE)
        out_ref[:, columns] = jnp.dot(rows, matrix_ref[:, columns], preferred_element_type=jnp.float32)


def other_kernel(turns, *refs):
    received_refs = refs[:turns]
    own_ref, weight_ref, *out_refs = refs[turns:]
    depth, width = weight_ref.shape
    rows = jnp.concatenate([received_ref[:, depth:] for received_ref in received_refs], axis=0)

    for start in range(0, width, TILE):
        columns = slice(start, start + TILE)
        part = jnp.dot(rows, weight_ref[:, columns], preferred_element_type=jnp.float32)
        total = own_ref[:, columns] + part
        start_row = 0
        for out_ref in out_refs:
            rows_here = out_ref.shape[0]
            out_ref[:, columns] = total[start_row : start_row + rows_here].astype(jnp.bfloat16)
            start_row += rows_here


def sum_kernel(split, pieces, place_ref, *refs):
    *refs, all_ref = refs
    returned_refs, own_ref, other_refs = refs[:-1-pieces], refs[-1-pieces], refs[-pieces:]
    block = returned_refs[0].shape[0]
    rows = own_ref.shape[0]
    for i, returned_ref in enumerate(returned_refs):
        all_ref[i * block : (i + 1) * block, :] = returned_ref[...]
    place = place_ref[...]
    place = jnp.concatenate([place[: split * block], place[(split + 1) * block :]], axis=0)
    total = lax.dot_general(
        place.astype(jnp.bfloat16),
        all_ref[...],
        (((0,), (0,)), ((), ())),
        preferred_element_type=jnp.float32,
    )
    own_ref[...] = total[:rows]
    start = 0
    for other_ref in other_refs:
        other_ref[...] = total[rows:, start : start + other_ref.shape[1]].astype(other_ref.dtype)
        start += other_ref.shape[1]


def last_kernel(pieces, own_ref, place_ref, *refs):
    other_refs, returned_refs, out_ref = refs[:pieces], refs[pieces:-1], refs[-1]
    slots = returned_refs[0].shape[0]
    total = own_ref[...] + jnp.concatenate([other_ref[...].astype(jnp.float32) for other_ref in other_refs], axis=1)
    for i, returned_ref in enumerate(returned_refs):
        total = total + lax.dot_general(
            place_ref[i * slots : (i + 1) * slots, :].astype(jnp.bfloat16),
            returned_ref[...],
            (((0,), (0,)), ((), ())),
            preferred_element_type=jnp.float32,
        )
    out_ref[...] = total.astype(jnp.bfloat16)


def local(
    expert_hidden,
    gate_scores,
    node_lists,
    expert_picks,
    routed_down,
    query_latent,
    query_rope,
    cache_latent,
    cache_rope,
    cache_lengths,
):
    node_count = lax.axis_size("node")
    lane_count = lax.axis_size("lane")
    row_count, _, hidden_width = expert_hidden.shape
    width = routed_down.shape[2]
    capacity = max(
        2, min(row_count // 2, 2 * ((row_count * NODES_TOP + node_count - 1) // node_count))
    )
    turns = node_count // lane_count
    block = lane_count * capacity
    slots = turns * block

    def other_core(value):
        return lax.ppermute(value, "lane", [(0, 1), (1, 0)])

    def meet(value, turn, across=0):
        pairs = []
        for node in range(node_count):
            for lane in range(lane_count):
                there = partner(node_count, node, number_of(node_count, lane_count, lane, turn))
                pairs.append((node * lane_count + lane, there * lane_count + (lane + across) % lane_count))
        return lax.ppermute(value, ("node", "lane"), pairs)

    whole = pl.BlockSpec(memory_space=pltpu.VMEM)
    outside = pl.BlockSpec(memory_space=pltpu.HBM)

    def in_hbm(value):
        return pltpu.with_memory_space_constraint(value, pltpu.HBM)

    def in_vmem(value):
        return pltpu.with_memory_space_constraint(value, pltpu.VMEM)

    def params(mib):
        return pltpu.CompilerParams(vmem_limit_bytes=mib * MIB)

    own_matrix = routed_down[0]
    mine = [gate_scores.T, node_lists.T, expert_picks.T, expert_hidden.reshape(-1, hidden_width)]
    theirs = [other_core(value) for value in mine]
    mine = pl.pallas_call(
        load_kernel,
        in_specs=[outside] * 4,
        out_specs=[whole] * 4,
        out_shape=[pltpu.VMEM(value.shape, value.dtype) for value in mine],
        scratch_shapes=[pltpu.SemaphoreType.DMA((4,))],
        compiler_params=params(1),
        name="load",
    )(*[in_hbm(value) for value in mine])
    sent_matrix, *_ = lax.optimization_barrier((own_matrix, *theirs, mine[0]))
    other_matrix = other_core(sent_matrix)
    split = turns // 2 - 1
    send = pl.pallas_call(
        functools.partial(pack_kernel, node_count, lane_count, capacity),
        in_specs=[whole] * 8,
        out_specs=[whole] * turns,
        out_shape=[jax.ShapeDtypeStruct((block, lane_count * hidden_width), jnp.bfloat16)] * turns,
        compiler_params=params(4),
        cost_estimate=pl.CostEstimate(flops=6 * 10**9, bytes_accessed=0, transcendentals=0),
        name="pack",
    )(*[in_vmem(value) for value in (*mine, *theirs)])
    received = [meet(value, turn) for turn, value in enumerate(send)]
    *attention, _ = lax.optimization_barrier(
        (query_latent, query_rope, cache_latent, cache_rope, cache_lengths, send[-1])
    )
    context = attend(*attention)
    *received, context = lax.optimization_barrier((*received, context))
    own_part = pl.pallas_call(
        own_kernel,
        in_specs=[whole] * (turns + 1),
        out_specs=whole,
        out_shape=jax.ShapeDtypeStruct((slots, width), jnp.float32),
        compiler_params=params(2),
        name="own",
    )(*received, in_vmem(own_matrix))
    pieces = [block] * split + [capacity] * lane_count + [block] * (turns - split - 1)
    output = pl.pallas_call(
        functools.partial(other_kernel, turns),
        in_specs=[whole] * (turns + 2),
        out_specs=[whole] * len(pieces),
        out_shape=[jax.ShapeDtypeStruct((rows, width), jnp.bfloat16) for rows in pieces],
        compiler_params=params(2),
        name="other",
    )(*received, in_vmem(own_part), in_vmem(other_matrix))
    returned = [meet(value, turn) for turn, value in enumerate(output[:split])]
    last = [meet(output[split + across], split, across) for across in range(lane_count)]
    returned += [meet(value, turn) for turn, value in enumerate(output[split + lane_count :], split + 1)]
    late, _ = lax.optimization_barrier((mine[1], output[-1]))
    place, split_place = pl.pallas_call(
        functools.partial(place_kernel, node_count, lane_count, capacity, split),
        in_specs=[whole] * 4,
        out_specs=[whole] * 2,
        out_shape=[
            jax.ShapeDtypeStruct((slots, lane_count * row_count), jnp.float32),
            jax.ShapeDtypeStruct((block, row_count), jnp.float32),
        ],
        compiler_params=params(2),
        name="place",
    )(*[in_vmem(value) for value in (late, mine[2], *theirs[1:3])])
    tiles = width // 128
    widths = [128 * ((i + 1) * tiles // 3 - i * tiles // 3) for i in range(3)]
    own, *others = pl.pallas_call(
        functools.partial(sum_kernel, split, len(widths)),
        in_specs=[whole] * turns,
        out_specs=[whole] * (1 + len(widths)),
        out_shape=[jax.ShapeDtypeStruct((row_count, width), jnp.float32)]
        + [jax.ShapeDtypeStruct((row_count, piece), jnp.bfloat16) for piece in widths],
        scratch_shapes=[pltpu.VMEM((slots - block, width), jnp.bfloat16)],
        compiler_params=params(8),
        cost_estimate=pl.CostEstimate(flops=0, bytes_accessed=0, transcendentals=0),
        name="sum",
    )(place, *returned)
    others = [in_vmem(other_core(value)) for value in others]
    moe_out = pl.pallas_call(
        functools.partial(last_kernel, len(widths)),
        in_specs=[whole] * (2 + len(widths) + lane_count),
        out_specs=whole,
        out_shape=jax.ShapeDtypeStruct((row_count, width), jnp.bfloat16),
        compiler_params=params(2),
        name="last",
    )(in_vmem(own), split_place, *others, *[in_vmem(value) for value in last])
    return (moe_out, context)


def solution(mesh):
    placed = (
        P(("groups", "node", "lane"), None, None),
        P(("groups", "node", "lane"), None),
        P(("groups", "node", "lane"), None),
        P(("groups", "node", "lane"), None),
        P(("node", "lane"), None, None),
        P(("groups", "node", "lane"), None, None),
        P(("groups", "node", "lane"), None),
        P(("groups", "node", "lane"), None, None),
        P(("groups", "node", "lane"), None, None),
        P(("groups", "node", "lane")),
    )
    return jax.shard_map(
        local,
        mesh=mesh,
        in_specs=placed,
        out_specs=(P(("groups", "node", "lane"), None), P(("groups", "node", "lane"), None, None)),
        check_vma=False,
    )
```

```python
import functools

import jax
import jax.numpy as jnp
from jax import lax
from jax.experimental import pallas as pl
from jax.experimental.pallas import tpu as pltpu
from jax.sharding import PartitionSpec as P

NODES_TOP = 4
MIB = 2**20
TILE = 512


score_scale = 192.0 ** (-0.5)
route_scale = 2.5


def attend_kernel(lengths_ref, latent_ref, rope_ref, keys_ref, rope_keys_ref, out_ref):
    row_count, head_count, _ = latent_ref.shape
    rope_width, position_count = rope_keys_ref.shape[1:]
    lanes = max(128, rope_width)
    heads = lanes // rope_width
    groups = rope_ref.shape[1] // lanes
    rope = rope_ref[...].astype(jnp.float32)
    rope = jnp.concatenate([rope[:, i * lanes : (i + 1) * lanes] for i in range(groups)], axis=0)
    shape = (row_count * head_count, groups * row_count)
    head = lax.rem(iota(shape, 0), head_count)
    picked = iota(shape, 1) == head // heads * row_count + iota(shape, 0) // head_count
    rope = exact(jnp.where(picked, 1.0, 0.0), rope)
    kept = iota(rope.shape, 1) // rope_width == lax.rem(iota(rope.shape, 0), heads)
    rope = jnp.where(kept, rope, 0.0).astype(jnp.bfloat16)
    scores = []
    for row in range(row_count):
        score = lax.dot_general(
            latent_ref[row], keys_ref[row], (((1,), (1,)), ((), ())), preferred_element_type=jnp.float32
        )
        rope_keys = jnp.concatenate([rope_keys_ref[row]] * heads, axis=0)
        score = score + jnp.dot(
            rope[row * head_count : (row + 1) * head_count], rope_keys, preferred_element_type=jnp.float32
        )
        valid = iota(score.shape, 1) < lengths_ref[row]
        scores.append(jnp.where(valid, score * score_scale, -jnp.inf))
    scores = jnp.concatenate(scores, axis=0)
    expd = jnp.exp(scores - jnp.max(scores, axis=-1, keepdims=True))
    probs = (expd / jnp.sum(expd, axis=-1, keepdims=True)).astype(jnp.bfloat16)
    for row in range(row_count):
        context = jnp.dot(
            probs[row * head_count : (row + 1) * head_count], keys_ref[row], preferred_element_type=jnp.float32
        )
        out_ref[row] = context.astype(jnp.bfloat16)


def attend(query_latent, query_rope, cache_latent, cache_rope, cache_lengths):
    return pl.pallas_call(
        attend_kernel,
        in_specs=[pl.BlockSpec(memory_space=pltpu.SMEM)] + [pl.BlockSpec(memory_space=pltpu.VMEM)] * 4,
        out_specs=pl.BlockSpec(memory_space=pltpu.VMEM),
        out_shape=jax.ShapeDtypeStruct(query_latent.shape, jnp.bfloat16),
        compiler_params=pltpu.CompilerParams(vmem_limit_bytes=8 * MIB),
        name="attend",
    )(cache_lengths, query_latent, query_rope, cache_latent, cache_rope)


def iota(shape, dim):
    return lax.broadcasted_iota(jnp.int32, shape, dim)


def exact(a, b):
    return jnp.dot(a.astype(jnp.bfloat16), b.astype(jnp.bfloat16), preferred_element_type=jnp.float32)


def meeting(node_count, a, b):
    return a ^ b if node_count & (node_count - 1) == 0 else (a + b) % node_count


def partner(node_count, a, number):
    return a ^ number if node_count & (node_count - 1) == 0 else (number - a) % node_count


def turn_of(node_count, lane_count, lane, number):
    half = node_count // 2
    far_turn = (number - half) // lane_count
    far_lane = lane_count - 1 - (number - half) % lane_count
    near_turn = (node_count - 1 - number) // lane_count
    turn = jnp.where(number >= half, far_turn, near_turn)
    return jnp.where(jnp.where(number >= half, far_lane, number % lane_count) == lane, turn, -1)


def number_of(node_count, lane_count, lane, turn):
    half = node_count // 2
    if turn < half // lane_count:
        return half + lane_count * turn + lane_count - 1 - lane
    return node_count - lane_count * (turn + 1) + lane


def load_kernel(*refs):
    *refs, sems = refs
    half = len(refs) // 2
    copies = [
        pltpu.make_async_copy(in_ref, out_ref, sems.at[i])
        for i, (in_ref, out_ref) in enumerate(zip(refs[:half], refs[half:]))
    ]
    for copy in copies:
        copy.start()
    for copy in copies:
        copy.wait()


def spread_of(pick_count, row_count):
    items = pick_count * row_count
    spread = iota((row_count, items), 1) // pick_count == iota((row_count, items), 0)
    return jnp.where(spread, 1.0, 0.0).astype(jnp.bfloat16)


def flat(values, spread):
    pick_count, _ = values.shape
    _, items = spread.shape
    own_pick = lax.rem(iota((pick_count, items), 1), pick_count) == iota((pick_count, items), 0)
    return jnp.sum(jnp.where(own_pick, exact(values, spread), 0.0), axis=0, keepdims=True)


def route(node_count, lane_count, lists, picks, spread):
    _, row_count = picks.shape
    _, items = spread.shape
    lane_here = lax.axis_index("lane")
    before = iota((row_count, row_count), 0) < iota((row_count, row_count), 1)
    nodes = iota((node_count, row_count), 0)
    choice = picks // lane_count
    order = lax.rem(picks - choice * lane_count - lane_here + lane_count, lane_count)
    node = jnp.zeros_like(picks)
    member = jnp.zeros((node_count, row_count), jnp.float32)
    for j in range(lists.shape[0]):
        node = jnp.where(choice == j, lists[j : j + 1, :], node)
        member = jnp.where(nodes == lists[j : j + 1, :], 1.0, member)
    earlier = exact(exact(member, jnp.where(before, 1.0, 0.0)), spread)
    both = flat((node * lane_count + order).astype(jnp.float32), spread).astype(jnp.int32)
    node = both // lane_count
    order = both - node * lane_count
    named = iota((node_count, items), 0) == node
    slot = jnp.sum(jnp.where(named, earlier, 0.0), axis=0, keepdims=True).astype(jnp.int32)
    return meeting(node_count, lax.axis_index("node"), node), slot, order


def target_of(node_count, lane_count, capacity, source, number, slot):
    turn = turn_of(node_count, lane_count, lax.axis_index("lane"), number)
    return jnp.where(turn >= 0, (turn * lane_count + source) * capacity + slot, -1)


def pack_kernel(node_count, lane_count, capacity, *refs):
    sources = [refs[4 * s : 4 * s + 4] for s in range(lane_count)]
    send_refs = refs[4 * lane_count :]
    block = lane_count * capacity
    slots = len(send_refs) * block
    hidden_width = sources[0][3].shape[1]
    spread = spread_of(*sources[0][0].shape)
    places = iota((slots, spread.shape[1]), 0)
    parts = [None] * lane_count
    for s, (scores_ref, lists_ref, picks_ref, hidden_ref) in enumerate(sources):
        scores = scores_ref[...]
        combine = (route_scale * scores / jnp.sum(scores, axis=0, keepdims=True)).astype(jnp.bfloat16)
        weight = flat(combine, spread)
        number, slot, order = route(node_count, lane_count, lists_ref[...], picks_ref[...], spread)
        at = places == target_of(node_count, lane_count, capacity, s, number, slot)
        hidden = hidden_ref[...]
        for q in range(lane_count):
            placing = jnp.where(at & (order == q), weight, 0.0).astype(jnp.bfloat16)
            part = jnp.dot(placing, hidden, preferred_element_type=jnp.float32)
            parts[q] = part if parts[q] is None else parts[q] + part
    for q in range(lane_count):
        columns = slice(q * hidden_width, (q + 1) * hidden_width)
        for turn, send_ref in enumerate(send_refs):
            send_ref[:, columns] = parts[q][turn * block : (turn + 1) * block].astype(jnp.bfloat16)


def place_kernel(node_count, lane_count, capacity, split, *refs):
    *refs, place_ref, split_ref = refs
    pick_count, row_count = refs[1].shape
    spread = spread_of(pick_count, row_count)
    items = pick_count * row_count

    def marked(at):
        marks = lax.dot_general(
            jnp.where(at, 1.0, 0.0).astype(jnp.bfloat16),
            spread,
            (((1,), (1,)), ((), ())),
            preferred_element_type=jnp.float32,
        )
        return jnp.where(marks > 0.0, 1.0, 0.0)

    for s in range(lane_count):
        lists_ref, picks_ref = refs[2 * s : 2 * s + 2]
        number, slot, _ = route(node_count, lane_count, lists_ref[...], picks_ref[...], spread)
        target = target_of(node_count, lane_count, capacity, s, number, slot)
        place_ref[:, s * row_count : (s + 1) * row_count] = marked(
            iota((place_ref.shape[0], items), 0) == target
        )
        if s == 0:
            for q in range(lane_count):
                lane = lax.rem(lax.axis_index("lane") + q, lane_count)
                there = number == number_of(node_count, lane_count, lane, split)
                split_ref[q * capacity : (q + 1) * capacity, :] = marked(
                    iota((capacity, items), 0) == jnp.where(there, slot, -1)
                )


def own_kernel(*refs):
    *received_refs, matrix_ref, out_ref = refs
    depth, width = matrix_ref.shape
    rows = jnp.concatenate([received_ref[:, :depth] for received_ref in received_refs], axis=0)
    for start in range(0, width, TILE):
        columns = slice(start, start + TILE)
        out_ref[:, columns] = jnp.dot(rows, matrix_ref[:, columns], preferred_element_type=jnp.float32)


def other_kernel(turns, *refs):
    received_refs = refs[:turns]
    own_ref, weight_ref, *out_refs = refs[turns:]
    depth, width = weight_ref.shape
    rows = jnp.concatenate([received_ref[:, depth:] for received_ref in received_refs], axis=0)

    for start in range(0, width, TILE):
        columns = slice(start, start + TILE)
        part = jnp.dot(rows, weight_ref[:, columns], preferred_element_type=jnp.float32)
        total = own_ref[:, columns] + part
        start_row = 0
        for out_ref in out_refs:
            rows_here = out_ref.shape[0]
            out_ref[:, columns] = total[start_row : start_row + rows_here].astype(jnp.bfloat16)
            start_row += rows_here


def sum_kernel(split, pieces, place_ref, *refs):
    *refs, all_ref = refs
    returned_refs, own_ref, other_refs = refs[:-1-pieces], refs[-1-pieces], refs[-pieces:]
    block = returned_refs[0].shape[0]
    rows = own_ref.shape[0]
    for i, returned_ref in enumerate(returned_refs):
        all_ref[i * block : (i + 1) * block, :] = returned_ref[...]
    place = place_ref[...]
    place = jnp.concatenate([place[: split * block], place[(split + 1) * block :]], axis=0)
    total = lax.dot_general(
        place.astype(jnp.bfloat16),
        all_ref[...],
        (((0,), (0,)), ((), ())),
        preferred_element_type=jnp.float32,
    )
    own_ref[...] = total[:rows]
    start = 0
    for other_ref in other_refs:
        other_ref[...] = total[rows:, start : start + other_ref.shape[1]].astype(other_ref.dtype)
        start += other_ref.shape[1]


def last_kernel(pieces, own_ref, place_ref, *refs):
    other_refs, returned_refs, (out_ref, rows_ref, sems) = refs[:pieces], refs[pieces:-3], refs[-3:]
    place = place_ref[...].astype(jnp.bfloat16)
    copies = []
    start = 0
    for i, other_ref in enumerate(other_refs):
        columns = slice(start, start + other_ref.shape[1])
        start = columns.stop
        returned = jnp.concatenate([returned_ref[:, columns] for returned_ref in returned_refs], axis=0)
        total = own_ref[:, columns] + other_ref[...].astype(jnp.float32)
        total = total + lax.dot_general(
            place, returned, (((0,), (0,)), ((), ())), preferred_element_type=jnp.float32
        )
        rows_ref[:, columns] = total.astype(jnp.bfloat16)
        copies.append(pltpu.make_async_copy(rows_ref.at[:, columns], out_ref.at[:, columns], sems.at[i]))
        copies[-1].start()
    for copy in copies:
        copy.wait()


def local(
    expert_hidden,
    gate_scores,
    node_lists,
    expert_picks,
    routed_down,
    query_latent,
    query_rope,
    cache_latent,
    cache_rope,
    cache_lengths,
):
    node_count = lax.axis_size("node")
    lane_count = lax.axis_size("lane")
    row_count, _, hidden_width = expert_hidden.shape
    width = routed_down.shape[2]
    capacity = max(
        2, min(row_count // 2, 2 * ((row_count * NODES_TOP + node_count - 1) // node_count))
    )
    turns = node_count // lane_count
    block = lane_count * capacity
    slots = turns * block

    def other_core(value):
        return lax.ppermute(value, "lane", [(0, 1), (1, 0)])

    def meet(value, turn, across=0):
        pairs = []
        for node in range(node_count):
            for lane in range(lane_count):
                there = partner(node_count, node, number_of(node_count, lane_count, lane, turn))
                pairs.append((node * lane_count + lane, there * lane_count + (lane + across) % lane_count))
        return lax.ppermute(value, ("node", "lane"), pairs)

    whole = pl.BlockSpec(memory_space=pltpu.VMEM)
    outside = pl.BlockSpec(memory_space=pltpu.HBM)

    def in_hbm(value):
        return pltpu.with_memory_space_constraint(value, pltpu.HBM)

    def in_vmem(value):
        return pltpu.with_memory_space_constraint(value, pltpu.VMEM)

    def params(mib):
        return pltpu.CompilerParams(vmem_limit_bytes=mib * MIB)

    own_matrix = routed_down[0]
    mine = [gate_scores.T, node_lists.T, expert_picks.T, expert_hidden.reshape(-1, hidden_width)]
    theirs = [other_core(value) for value in mine]
    mine = pl.pallas_call(
        load_kernel,
        in_specs=[outside] * 4,
        out_specs=[whole] * 4,
        out_shape=[pltpu.VMEM(value.shape, value.dtype) for value in mine],
        scratch_shapes=[pltpu.SemaphoreType.DMA((4,))],
        compiler_params=params(1),
        name="load",
    )(*[in_hbm(value) for value in mine])
    sent_matrix, *_ = lax.optimization_barrier((own_matrix, *theirs, mine[0]))
    other_matrix = other_core(sent_matrix)
    split = turns // 2 - 1
    send = pl.pallas_call(
        functools.partial(pack_kernel, node_count, lane_count, capacity),
        in_specs=[whole] * 8,
        out_specs=[whole] * turns,
        out_shape=[jax.ShapeDtypeStruct((block, lane_count * hidden_width), jnp.bfloat16)] * turns,
        compiler_params=params(4),
        cost_estimate=pl.CostEstimate(flops=6 * 10**9, bytes_accessed=0, transcendentals=0),
        name="pack",
    )(*[in_vmem(value) for value in (*mine, *theirs)])
    received = [meet(value, turn) for turn, value in enumerate(send)]
    *attention, _ = lax.optimization_barrier(
        (query_latent, query_rope, cache_latent, cache_rope, cache_lengths, send[-1])
    )
    context = attend(*attention)
    *received, context = lax.optimization_barrier((*received, context))
    own_part = pl.pallas_call(
        own_kernel,
        in_specs=[whole] * (turns + 1),
        out_specs=whole,
        out_shape=jax.ShapeDtypeStruct((slots, width), jnp.float32),
        compiler_params=params(2),
        name="own",
    )(*received, in_vmem(own_matrix))
    pieces = [block] * split + [capacity] * lane_count + [block] * (turns - split - 1)
    output = pl.pallas_call(
        functools.partial(other_kernel, turns),
        in_specs=[whole] * (turns + 2),
        out_specs=[whole] * len(pieces),
        out_shape=[jax.ShapeDtypeStruct((rows, width), jnp.bfloat16) for rows in pieces],
        compiler_params=params(2),
        name="other",
    )(*received, in_vmem(own_part), in_vmem(other_matrix))
    returned = [meet(value, turn) for turn, value in enumerate(output[:split])]
    last = [meet(output[split + across], split, across) for across in range(lane_count)]
    returned += [meet(value, turn) for turn, value in enumerate(output[split + lane_count :], split + 1)]
    late, _ = lax.optimization_barrier((mine[1], output[-1]))
    place, split_place = pl.pallas_call(
        functools.partial(place_kernel, node_count, lane_count, capacity, split),
        in_specs=[whole] * 4,
        out_specs=[whole] * 2,
        out_shape=[
            jax.ShapeDtypeStruct((slots, lane_count * row_count), jnp.float32),
            jax.ShapeDtypeStruct((block, row_count), jnp.float32),
        ],
        compiler_params=params(2),
        name="place",
    )(*[in_vmem(value) for value in (late, mine[2], *theirs[1:3])])
    tiles = width // 128
    widths = [128 * ((i + 1) * tiles // 3 - i * tiles // 3) for i in range(3)]
    own, *others = pl.pallas_call(
        functools.partial(sum_kernel, split, len(widths)),
        in_specs=[whole] * turns,
        out_specs=[whole] * (1 + len(widths)),
        out_shape=[jax.ShapeDtypeStruct((row_count, width), jnp.float32)]
        + [jax.ShapeDtypeStruct((row_count, piece), jnp.bfloat16) for piece in widths],
        scratch_shapes=[pltpu.VMEM((slots - block, width), jnp.bfloat16)],
        compiler_params=params(8),
        cost_estimate=pl.CostEstimate(flops=0, bytes_accessed=0, transcendentals=0),
        name="sum",
    )(place, *returned)
    others = [in_vmem(other_core(value)) for value in others]
    moe_out = pl.pallas_call(
        functools.partial(last_kernel, len(widths)),
        in_specs=[whole] * (2 + len(widths) + lane_count),
        out_specs=pl.BlockSpec(memory_space=pl.ANY),
        out_shape=jax.ShapeDtypeStruct((row_count, width), jnp.bfloat16),
        scratch_shapes=[
            pltpu.VMEM((row_count, width), jnp.bfloat16),
            pltpu.SemaphoreType.DMA((len(widths),)),
        ],
        compiler_params=params(2),
        name="last",
    )(in_vmem(own), split_place, *others, *[in_vmem(value) for value in last])
    return (moe_out, context)


def solution(mesh):
    placed = (
        P(("groups", "node", "lane"), None, None),
        P(("groups", "node", "lane"), None),
        P(("groups", "node", "lane"), None),
        P(("groups", "node", "lane"), None),
        P(("node", "lane"), None, None),
        P(("groups", "node", "lane"), None, None),
        P(("groups", "node", "lane"), None),
        P(("groups", "node", "lane"), None, None),
        P(("groups", "node", "lane"), None, None),
        P(("groups", "node", "lane")),
    )
    return jax.shard_map(
        local,
        mesh=mesh,
        in_specs=placed,
        out_specs=(P(("groups", "node", "lane"), None), P(("groups", "node", "lane"), None, None)),
        check_vma=False,
    )
```

```python
import functools

import jax
import jax.numpy as jnp
from jax import lax
from jax.experimental import pallas as pl
from jax.experimental.pallas import tpu as pltpu
from jax.sharding import PartitionSpec as P

NODES_TOP = 4
MIB = 2**20
TILE = 512


score_scale = 192.0 ** (-0.5)
route_scale = 2.5


def attend_kernel(lengths_ref, latent_ref, rope_ref, keys_ref, rope_keys_ref, out_ref):
    row_count, head_count, _ = latent_ref.shape
    rope_width, position_count = rope_keys_ref.shape[1:]
    lanes = max(128, rope_width)
    heads = lanes // rope_width
    groups = rope_ref.shape[1] // lanes
    rope = rope_ref[...].astype(jnp.float32)
    rope = jnp.concatenate([rope[:, i * lanes : (i + 1) * lanes] for i in range(groups)], axis=0)
    shape = (row_count * head_count, groups * row_count)
    head = lax.rem(iota(shape, 0), head_count)
    picked = iota(shape, 1) == head // heads * row_count + iota(shape, 0) // head_count
    rope = exact(jnp.where(picked, 1.0, 0.0), rope)
    kept = iota(rope.shape, 1) // rope_width == lax.rem(iota(rope.shape, 0), heads)
    rope = jnp.where(kept, rope, 0.0).astype(jnp.bfloat16)
    scores = []
    for row in range(row_count):
        score = lax.dot_general(
            latent_ref[row], keys_ref[row], (((1,), (1,)), ((), ())), preferred_element_type=jnp.float32
        )
        rope_keys = jnp.concatenate([rope_keys_ref[row]] * heads, axis=0)
        score = score + jnp.dot(
            rope[row * head_count : (row + 1) * head_count], rope_keys, preferred_element_type=jnp.float32
        )
        valid = iota(score.shape, 1) < lengths_ref[row]
        scores.append(jnp.where(valid, score * score_scale, -jnp.inf))
    scores = jnp.concatenate(scores, axis=0)
    expd = jnp.exp(scores - jnp.max(scores, axis=-1, keepdims=True))
    probs = (expd / jnp.sum(expd, axis=-1, keepdims=True)).astype(jnp.bfloat16)
    for row in range(row_count):
        context = jnp.dot(
            probs[row * head_count : (row + 1) * head_count], keys_ref[row], preferred_element_type=jnp.float32
        )
        out_ref[row] = context.astype(jnp.bfloat16)


def attend(query_latent, query_rope, cache_latent, cache_rope, cache_lengths):
    return pl.pallas_call(
        attend_kernel,
        in_specs=[pl.BlockSpec(memory_space=pltpu.SMEM)] + [pl.BlockSpec(memory_space=pltpu.VMEM)] * 4,
        out_specs=pl.BlockSpec(memory_space=pltpu.VMEM),
        out_shape=jax.ShapeDtypeStruct(query_latent.shape, jnp.bfloat16),
        compiler_params=pltpu.CompilerParams(vmem_limit_bytes=8 * MIB),
        name="attend",
    )(cache_lengths, query_latent, query_rope, cache_latent, cache_rope)


def iota(shape, dim):
    return lax.broadcasted_iota(jnp.int32, shape, dim)


def exact(a, b):
    return jnp.dot(a.astype(jnp.bfloat16), b.astype(jnp.bfloat16), preferred_element_type=jnp.float32)


def meeting(node_count, a, b):
    return a ^ b if node_count & (node_count - 1) == 0 else (a + b) % node_count


def partner(node_count, a, number):
    return a ^ number if node_count & (node_count - 1) == 0 else (number - a) % node_count


def turn_of(node_count, lane_count, lane, number):
    half = node_count // 2
    far_turn = (number - half) // lane_count
    far_lane = (number - half + lane_count - 1 + far_turn * (lane_count - 1)) % lane_count
    near_turn = (node_count - 1 - number) // lane_count
    turn = jnp.where(number >= half, far_turn, near_turn)
    return jnp.where(jnp.where(number >= half, far_lane, number % lane_count) == lane, turn, -1)


def number_of(node_count, lane_count, lane, turn):
    half = node_count // 2
    if turn < half // lane_count:
        return half + lane_count * turn + (turn + 1 + lane) % lane_count
    return node_count - lane_count * (turn + 1) + lane


def load_kernel(*refs):
    *refs, sems = refs
    half = len(refs) // 2
    copies = [
        pltpu.make_async_copy(in_ref, out_ref, sems.at[i])
        for i, (in_ref, out_ref) in enumerate(zip(refs[:half], refs[half:]))
    ]
    for copy in copies:
        copy.start()
    for copy in copies:
        copy.wait()


def spread_of(pick_count, row_count):
    items = pick_count * row_count
    spread = iota((row_count, items), 1) // pick_count == iota((row_count, items), 0)
    return jnp.where(spread, 1.0, 0.0).astype(jnp.bfloat16)


def flat(values, spread):
    pick_count, _ = values.shape
    _, items = spread.shape
    own_pick = lax.rem(iota((pick_count, items), 1), pick_count) == iota((pick_count, items), 0)
    return jnp.sum(jnp.where(own_pick, exact(values, spread), 0.0), axis=0, keepdims=True)


def route(node_count, lane_count, lists, picks, spread):
    _, row_count = picks.shape
    _, items = spread.shape
    lane_here = lax.axis_index("lane")
    before = iota((row_count, row_count), 0) < iota((row_count, row_count), 1)
    nodes = iota((node_count, row_count), 0)
    choice = picks // lane_count
    order = lax.rem(picks - choice * lane_count - lane_here + lane_count, lane_count)
    node = jnp.zeros_like(picks)
    member = jnp.zeros((node_count, row_count), jnp.float32)
    for j in range(lists.shape[0]):
        node = jnp.where(choice == j, lists[j : j + 1, :], node)
        member = jnp.where(nodes == lists[j : j + 1, :], 1.0, member)
    earlier = exact(exact(member, jnp.where(before, 1.0, 0.0)), spread)
    both = flat((node * lane_count + order).astype(jnp.float32), spread).astype(jnp.int32)
    node = both // lane_count
    order = both - node * lane_count
    named = iota((node_count, items), 0) == node
    slot = jnp.sum(jnp.where(named, earlier, 0.0), axis=0, keepdims=True).astype(jnp.int32)
    return meeting(node_count, lax.axis_index("node"), node), slot, order


def target_of(node_count, lane_count, capacity, source, number, slot):
    turn = turn_of(node_count, lane_count, lax.axis_index("lane"), number)
    return jnp.where(turn >= 0, (turn * lane_count + source) * capacity + slot, -1)


def pack_kernel(node_count, lane_count, capacity, *refs):
    sources = [refs[4 * s : 4 * s + 4] for s in range(lane_count)]
    send_refs = refs[4 * lane_count :]
    block = lane_count * capacity
    slots = len(send_refs) * block
    hidden_width = sources[0][3].shape[1]
    spread = spread_of(*sources[0][0].shape)
    places = iota((slots, spread.shape[1]), 0)
    parts = [None] * lane_count
    for s, (scores_ref, lists_ref, picks_ref, hidden_ref) in enumerate(sources):
        scores = scores_ref[...]
        combine = (route_scale * scores / jnp.sum(scores, axis=0, keepdims=True)).astype(jnp.bfloat16)
        weight = flat(combine, spread)
        number, slot, order = route(node_count, lane_count, lists_ref[...], picks_ref[...], spread)
        at = places == target_of(node_count, lane_count, capacity, s, number, slot)
        hidden = hidden_ref[...]
        for q in range(lane_count):
            placing = jnp.where(at & (order == q), weight, 0.0).astype(jnp.bfloat16)
            part = jnp.dot(placing, hidden, preferred_element_type=jnp.float32)
            parts[q] = part if parts[q] is None else parts[q] + part
    for q in range(lane_count):
        columns = slice(q * hidden_width, (q + 1) * hidden_width)
        for turn, send_ref in enumerate(send_refs):
            send_ref[:, columns] = parts[q][turn * block : (turn + 1) * block].astype(jnp.bfloat16)


def place_kernel(node_count, lane_count, capacity, split, *refs):
    *refs, place_ref, split_ref = refs
    pick_count, row_count = refs[1].shape
    spread = spread_of(pick_count, row_count)
    items = pick_count * row_count

    def marked(at):
        marks = lax.dot_general(
            jnp.where(at, 1.0, 0.0).astype(jnp.bfloat16),
            spread,
            (((1,), (1,)), ((), ())),
            preferred_element_type=jnp.float32,
        )
        return jnp.where(marks > 0.0, 1.0, 0.0)

    for s in range(lane_count):
        lists_ref, picks_ref = refs[2 * s : 2 * s + 2]
        number, slot, _ = route(node_count, lane_count, lists_ref[...], picks_ref[...], spread)
        target = target_of(node_count, lane_count, capacity, s, number, slot)
        place_ref[:, s * row_count : (s + 1) * row_count] = marked(
            iota((place_ref.shape[0], items), 0) == target
        )
        if s == 0:
            for q in range(lane_count):
                lane = lax.rem(lax.axis_index("lane") + q, lane_count)
                there = number == number_of(node_count, lane_count, lane, split)
                split_ref[q * capacity : (q + 1) * capacity, :] = marked(
                    iota((capacity, items), 0) == jnp.where(there, slot, -1)
                )


def own_kernel(*refs):
    *received_refs, matrix_ref, out_ref = refs
    depth, width = matrix_ref.shape
    rows = jnp.concatenate([received_ref[:, :depth] for received_ref in received_refs], axis=0)
    for start in range(0, width, TILE):
        columns = slice(start, start + TILE)
        out_ref[:, columns] = jnp.dot(rows, matrix_ref[:, columns], preferred_element_type=jnp.float32)


def other_kernel(turns, *refs):
    received_refs = refs[:turns]
    own_ref, weight_ref, *out_refs = refs[turns:]
    depth, width = weight_ref.shape
    rows = jnp.concatenate([received_ref[:, depth:] for received_ref in received_refs], axis=0)

    for start in range(0, width, TILE):
        columns = slice(start, start + TILE)
        part = jnp.dot(rows, weight_ref[:, columns], preferred_element_type=jnp.float32)
        total = own_ref[:, columns] + part
        start_row = 0
        for out_ref in out_refs:
            rows_here = out_ref.shape[0]
            out_ref[:, columns] = total[start_row : start_row + rows_here].astype(jnp.bfloat16)
            start_row += rows_here


def sum_kernel(split, pieces, place_ref, *refs):
    *refs, all_ref = refs
    returned_refs, own_ref, other_refs = refs[:-1-pieces], refs[-1-pieces], refs[-pieces:]
    block = returned_refs[0].shape[0]
    rows = own_ref.shape[0]
    for i, returned_ref in enumerate(returned_refs):
        all_ref[i * block : (i + 1) * block, :] = returned_ref[...]
    place = place_ref[...]
    place = jnp.concatenate([place[: split * block], place[(split + 1) * block :]], axis=0)
    total = lax.dot_general(
        place.astype(jnp.bfloat16),
        all_ref[...],
        (((0,), (0,)), ((), ())),
        preferred_element_type=jnp.float32,
    )
    own_ref[...] = total[:rows]
    start = 0
    for other_ref in other_refs:
        other_ref[...] = total[rows:, start : start + other_ref.shape[1]].astype(other_ref.dtype)
        start += other_ref.shape[1]


def last_kernel(pieces, own_ref, place_ref, *refs):
    other_refs, returned_refs, (out_ref, rows_ref, sems) = refs[:pieces], refs[pieces:-3], refs[-3:]
    place = place_ref[...].astype(jnp.bfloat16)
    copies = []
    start = 0
    for i, other_ref in enumerate(other_refs):
        columns = slice(start, start + other_ref.shape[1])
        start = columns.stop
        returned = jnp.concatenate([returned_ref[:, columns] for returned_ref in returned_refs], axis=0)
        total = own_ref[:, columns] + other_ref[...].astype(jnp.float32)
        total = total + lax.dot_general(
            place, returned, (((0,), (0,)), ((), ())), preferred_element_type=jnp.float32
        )
        rows_ref[:, columns] = total.astype(jnp.bfloat16)
        copies.append(pltpu.make_async_copy(rows_ref.at[:, columns], out_ref.at[:, columns], sems.at[i]))
        copies[-1].start()
    for copy in copies:
        copy.wait()


def local(
    expert_hidden,
    gate_scores,
    node_lists,
    expert_picks,
    routed_down,
    query_latent,
    query_rope,
    cache_latent,
    cache_rope,
    cache_lengths,
):
    node_count = lax.axis_size("node")
    lane_count = lax.axis_size("lane")
    row_count, _, hidden_width = expert_hidden.shape
    width = routed_down.shape[2]
    capacity = max(
        2, min(row_count // 2, 2 * ((row_count * NODES_TOP + node_count - 1) // node_count))
    )
    turns = node_count // lane_count
    block = lane_count * capacity
    slots = turns * block

    def other_core(value):
        return lax.ppermute(value, "lane", [(0, 1), (1, 0)])

    def meet(value, turn, across=0):
        pairs = []
        for node in range(node_count):
            for lane in range(lane_count):
                there = partner(node_count, node, number_of(node_count, lane_count, lane, turn))
                pairs.append((node * lane_count + lane, there * lane_count + (lane + across) % lane_count))
        return lax.ppermute(value, ("node", "lane"), pairs)

    whole = pl.BlockSpec(memory_space=pltpu.VMEM)
    outside = pl.BlockSpec(memory_space=pltpu.HBM)

    def in_hbm(value):
        return pltpu.with_memory_space_constraint(value, pltpu.HBM)

    def in_vmem(value):
        return pltpu.with_memory_space_constraint(value, pltpu.VMEM)

    def params(mib):
        return pltpu.CompilerParams(vmem_limit_bytes=mib * MIB)

    own_matrix = routed_down[0]
    mine = [gate_scores.T, node_lists.T, expert_picks.T, expert_hidden.reshape(-1, hidden_width)]
    theirs = [other_core(value) for value in mine]
    mine = pl.pallas_call(
        load_kernel,
        in_specs=[outside] * 4,
        out_specs=[whole] * 4,
        out_shape=[pltpu.VMEM(value.shape, value.dtype) for value in mine],
        scratch_shapes=[pltpu.SemaphoreType.DMA((4,))],
        compiler_params=params(1),
        name="load",
    )(*[in_hbm(value) for value in mine])
    sent_matrix, *_ = lax.optimization_barrier((own_matrix, *theirs, mine[0]))
    other_matrix = other_core(sent_matrix)
    split = turns // 2 - 1
    send = pl.pallas_call(
        functools.partial(pack_kernel, node_count, lane_count, capacity),
        in_specs=[whole] * 8,
        out_specs=[whole] * turns,
        out_shape=[jax.ShapeDtypeStruct((block, lane_count * hidden_width), jnp.bfloat16)] * turns,
        compiler_params=params(4),
        cost_estimate=pl.CostEstimate(flops=6 * 10**9, bytes_accessed=0, transcendentals=0),
        name="pack",
    )(*[in_vmem(value) for value in (*mine, *theirs)])
    received = [meet(value, turn) for turn, value in enumerate(send)]
    *attention, _ = lax.optimization_barrier(
        (query_latent, query_rope, cache_latent, cache_rope, cache_lengths, send[-1])
    )
    context = attend(*attention)
    *received, context = lax.optimization_barrier((*received, context))
    own_part = pl.pallas_call(
        own_kernel,
        in_specs=[whole] * (turns + 1),
        out_specs=whole,
        out_shape=jax.ShapeDtypeStruct((slots, width), jnp.float32),
        compiler_params=params(2),
        name="own",
    )(*received, in_vmem(own_matrix))
    pieces = [block] * split + [capacity] * lane_count + [block] * (turns - split - 1)
    output = pl.pallas_call(
        functools.partial(other_kernel, turns),
        in_specs=[whole] * (turns + 2),
        out_specs=[whole] * len(pieces),
        out_shape=[jax.ShapeDtypeStruct((rows, width), jnp.bfloat16) for rows in pieces],
        compiler_params=params(2),
        name="other",
    )(*received, in_vmem(own_part), in_vmem(other_matrix))
    returned = [meet(value, turn) for turn, value in enumerate(output[:split])]
    last = [meet(output[split + across], split, across) for across in range(lane_count)]
    returned += [meet(value, turn) for turn, value in enumerate(output[split + lane_count :], split + 1)]
    late, _ = lax.optimization_barrier((mine[1], output[-1]))
    place, split_place = pl.pallas_call(
        functools.partial(place_kernel, node_count, lane_count, capacity, split),
        in_specs=[whole] * 4,
        out_specs=[whole] * 2,
        out_shape=[
            jax.ShapeDtypeStruct((slots, lane_count * row_count), jnp.float32),
            jax.ShapeDtypeStruct((block, row_count), jnp.float32),
        ],
        compiler_params=params(2),
        name="place",
    )(*[in_vmem(value) for value in (late, mine[2], *theirs[1:3])])
    tiles = width // 128
    widths = [128 * ((i + 1) * tiles // 3 - i * tiles // 3) for i in range(3)]
    own, *others = pl.pallas_call(
        functools.partial(sum_kernel, split, len(widths)),
        in_specs=[whole] * turns,
        out_specs=[whole] * (1 + len(widths)),
        out_shape=[jax.ShapeDtypeStruct((row_count, width), jnp.float32)]
        + [jax.ShapeDtypeStruct((row_count, piece), jnp.bfloat16) for piece in widths],
        scratch_shapes=[pltpu.VMEM((slots - block, width), jnp.bfloat16)],
        compiler_params=params(8),
        cost_estimate=pl.CostEstimate(flops=0, bytes_accessed=0, transcendentals=0),
        name="sum",
    )(place, *returned)
    others = [in_vmem(other_core(value)) for value in others]
    moe_out = pl.pallas_call(
        functools.partial(last_kernel, len(widths)),
        in_specs=[whole] * (2 + len(widths) + lane_count),
        out_specs=pl.BlockSpec(memory_space=pl.ANY),
        out_shape=jax.ShapeDtypeStruct((row_count, width), jnp.bfloat16),
        scratch_shapes=[
            pltpu.VMEM((row_count, width), jnp.bfloat16),
            pltpu.SemaphoreType.DMA((len(widths),)),
        ],
        compiler_params=params(2),
        name="last",
    )(in_vmem(own), split_place, *others, *[in_vmem(value) for value in last])
    return (moe_out, context)


def solution(mesh):
    placed = (
        P(("groups", "node", "lane"), None, None),
        P(("groups", "node", "lane"), None),
        P(("groups", "node", "lane"), None),
        P(("groups", "node", "lane"), None),
        P(("node", "lane"), None, None),
        P(("groups", "node", "lane"), None, None),
        P(("groups", "node", "lane"), None),
        P(("groups", "node", "lane"), None, None),
        P(("groups", "node", "lane"), None, None),
        P(("groups", "node", "lane")),
    )
    return jax.shard_map(
        local,
        mesh=mesh,
        in_specs=placed,
        out_specs=(P(("groups", "node", "lane"), None), P(("groups", "node", "lane"), None, None)),
        check_vma=False,
    )
```
